128 devices in a mesh: row: 8 (over y, core), col: 16 (over x, z).
Axes of the slice: x: 4, y: 4, z: 4, core: 2. Of those that a mesh axis runs over, the one named last changes fastest.
Arguments:
- object_slab: float32 [2, 4096, 8192], P(None, 'row', 'col'), may hold values from -15 to 15
- probe_field: float32 [2, 4, 256, 256], replicated, may hold values from -6 to 6
- patterns: float32 [128, 4, 256, 256], P(('row', 'col')), may hold values from 0 to 3
- offsets: int32 [128, 4, 2], P(('row', 'col')), may hold values from 0 to 511
- counts: int32 [128], replicated, may hold values from 1 to 4, 176 in all
Outputs:
- new_object: float32 [2, 4096, 8192], P(None, 'row', 'col')
- new_probe: float32 [2, 4, 256, 256], replicated
- loss_mean: float32 [], replicated
The draws below stay inside these ranges and needn't reach their ends.
Inputs may be any that keep to these rules, and one draw needn't show every extreme that they name: The counts sum to 176; some tile owns exactly 4 positions. `offsets`: only the first counts[t] slots of tile t are scan positions.
All inputs are finite; a program needn't handle non-finite values.
Results may differ from the reference program's by a relative error of at most 0.0003.
Values sent between devices are 32-bit elements; how exact they have to be, the bound alone decides.
A program may use at most 128 MiB of HBM per device.

```python
import math
import jax
import jax.numpy as jnp
import numpy as np
from jax import lax

P_SIZE = 256
MODES = 4
TILE = 512
SLOTS = 4
LIVE = 176
NY = 4096
NX = 8192
N_COL = 16
DEVICES = 128


def draw_object_slab(key, part):
    key = jax.random.fold_in(key, 11)
    key_values = jax.random.fold_in(key, 1)
    key_rows = jax.random.fold_in(key, 2)
    key_cols = jax.random.fold_in(key, 3)
    values = jnp.clip(jax.random.normal(key_values, (2, NY, NX), jnp.float32), -6.0, 6.0)
    row_scale = jnp.exp(jax.random.uniform(key_rows, (NY,), jnp.float32, 0.0, math.log(1.8)))
    col_scale = jnp.exp(jax.random.uniform(key_cols, (NX,), jnp.float32, 0.0, math.log(1.8)))
    tile_row = jnp.arange(NY, dtype=jnp.int32) // TILE
    tile_col = jnp.arange(NX, dtype=jnp.int32) // TILE
    tile_number = tile_row[:, None] * (NX // TILE) + tile_col[None, :]
    spread = max(NY // TILE * (NX // TILE) - 1, 1)
    trend = jnp.exp(math.log(3.0) * tile_number.astype(jnp.float32) / spread)
    return 0.25 * values * trend[None] * row_scale[None, :, None] * col_scale[None, None, :]


def with_ends(array, rng, low, high):
    place = [jax.random.randint(jax.random.fold_in(rng, axis), (), 0, length) for axis, length in enumerate(array.shape)]
    longest = array.shape.index(max(array.shape))
    next_to = place[:longest] + [(place[longest] + 1) % array.shape[longest]] + place[longest + 1:]
    return array.at[tuple(place)].set(low).at[tuple(next_to)].set(high)


def shard_levels(key, extent, split, low, high):
    gain = 1.0
    for dim, parts in split:
        draws = jax.random.uniform(jax.random.fold_in(jax.random.fold_in(key, 6), dim), (parts,), jnp.float32, low / len(split), high / len(split))
        gain = gain * jnp.repeat(jnp.exp(draws), extent[dim] // parts).reshape((-1,) + (1,) * (len(extent) - 1 - dim))
    return gain


def length_profile(count, total, limit, skew):
    loads = [(1 << 20) // math.isqrt(rank ** skew) + 1 for rank in range(2, count + 1)]
    rest, holding = total - limit - (count - 1), [1] * (count - 1)
    while rest > 0:
        free = [i for i in range(count - 1) if holding[i] < limit]
        whole, budget = sum([loads[i] for i in free]), rest
        for i in free:
            more = min(limit - holding[i], max(1, budget * loads[i] // whole), rest)
            holding[i] = holding[i] + more
            rest = rest - more
    return np.array([limit] + holding)


def uneven_parts(rng, amount, total, bound, slope):
    if amount == 2:
        one = jax.random.randint(rng, (), max(1, total - bound), min(bound, total - 1) + 1)
        return jnp.stack([one, total - one])
    sizes = jnp.asarray(length_profile(amount, total, bound, slope), jnp.int32)
    couples = (amount - 1) // 2
    donor, sink = sizes[1:1 + 2 * couples:2], sizes[2:2 + 2 * couples:2]
    margin = jnp.minimum(donor - 1, bound - sink)
    moved = jax.random.randint(jax.random.fold_in(rng, 1), (couples,), 0, 1 << 20) % (margin + 1)
    sizes = sizes.at[1:1 + 2 * couples:2].set(donor - moved).at[2:2 + 2 * couples:2].set(sink + moved)
    return sizes[jax.random.permutation(jax.random.fold_in(rng, 2), amount)]


def bell_draw(stream_key, shape, scale, limit, held_as=jnp.bfloat16):
    return jnp.clip(scale * jax.random.normal(stream_key, shape, jnp.float32), -limit, limit).astype(held_as)


def setup_inputs(seed: int = 0) -> dict:
    arg_keys = jax.random.split(jax.random.key(seed), 6)
    object_slab = draw_object_slab(jax.random.fold_in(arg_keys[5], 71), 0)
    probe_field = bell_draw(arg_keys[1], (2, MODES, P_SIZE, P_SIZE), 0.4, 6.0, jnp.float32)
    patterns = jnp.clip(3.0 * jax.random.uniform(arg_keys[2], (DEVICES, SLOTS, P_SIZE, P_SIZE), jnp.float32) ** shard_levels(arg_keys[2], (DEVICES, SLOTS, P_SIZE, P_SIZE), ((0, 128),), -0.2, 0.2), 0.0, 3.0)
    offsets = with_ends(jax.random.randint(arg_keys[3], (DEVICES, SLOTS, 2), 0, TILE), jax.random.fold_in(arg_keys[3], 1), 0, TILE - 1).astype(jnp.int32)
    counts = uneven_parts(arg_keys[4], DEVICES, LIVE, SLOTS, 2).astype(jnp.int32)
    return {"object_slab": object_slab, "probe_field": probe_field, "patterns": patterns, "offsets": offsets, "counts": counts}


def reference(object_slab, probe_field, patterns, offsets, counts):
    pixels = probe_field.shape[-1]
    padded = jnp.pad(object_slab, ((0, 0), (0, pixels), (0, pixels)))
    object_field = padded[0] + 1j * padded[1]
    probe_modes = probe_field[0] + 1j * probe_field[1]
    flat_patterns = patterns.reshape(-1, pixels, pixels)
    flat_offsets = offsets.reshape(-1, 2)
    number = jnp.arange(flat_offsets.shape[0], dtype=jnp.int32)
    device = number // SLOTS
    slot_index = number % SLOTS

    def visit_position(carried, scan_item):
        grad_field, grad_modes, loss_sum = carried
        pattern, offset, owner_tile, slot_place = scan_item
        live_mask = (slot_place < counts[owner_tile]).astype(jnp.float32)
        corner_row = (owner_tile // N_COL) * TILE + offset[0]
        corner_col = (owner_tile % N_COL) * TILE + offset[1]
        obj_patch = lax.dynamic_slice(object_field, (corner_row, corner_col), (pixels, pixels))
        spectra = jnp.fft.fft2(probe_modes * obj_patch[None], norm="ortho")
        intensity = jnp.sum(jnp.real(spectra) * jnp.real(spectra) + jnp.imag(spectra) * jnp.imag(spectra), axis=0)
        residual = (intensity - pattern) * live_mask
        back_wave = jnp.fft.ifft2(residual[None] * spectra, norm="ortho")
        patch_grad = jnp.sum(jnp.conj(probe_modes) * back_wave, axis=0)
        current = lax.dynamic_slice(grad_field, (corner_row, corner_col), (pixels, pixels))
        grad_field = lax.dynamic_update_slice(grad_field, current + patch_grad, (corner_row, corner_col))
        grad_modes = grad_modes + jnp.conj(obj_patch)[None] * back_wave
        loss_sum = loss_sum + 0.5 * jnp.sum(residual * residual)
        return (grad_field, grad_modes, loss_sum), None

    start = (jnp.zeros_like(object_field), jnp.zeros_like(probe_modes), jnp.zeros((), jnp.float32))
    (grad_field, grad_modes, loss_sum), _ = lax.scan(visit_position, start, (flat_patterns, flat_offsets, device, slot_index))
    obj_grad = grad_field[: object_slab.shape[1], : object_slab.shape[2]]
    probe_peak = jnp.max(jnp.sum(probe_field[0] * probe_field[0] + probe_field[1] * probe_field[1], axis=0))
    object_peak = jnp.max(object_slab[0] * object_slab[0] + object_slab[1] * object_slab[1])
    new_object = object_slab - jnp.stack([jnp.real(obj_grad), jnp.imag(obj_grad)]) / probe_peak
    new_probe = probe_field - jnp.stack([jnp.real(grad_modes), jnp.imag(grad_modes)]) / object_peak
    scans = jnp.sum(counts).astype(jnp.float32) * (pixels * pixels)
    return new_object, new_probe, loss_sum / scans
```

```python
import math

import jax
import jax.numpy as jnp
import ml_dtypes
import numpy as np
from jax import lax
from jax.experimental import pallas as pl
from jax.experimental.pallas import tpu as pltpu
from jax.sharding import PartitionSpec as P

N = 256
H = 128

def split(x):
    hi = x.astype(jnp.bfloat16)
    lo = (x - hi.astype(jnp.float32)).astype(jnp.bfloat16)
    return hi, lo

def tables():
    k = np.arange(H)[:, None]
    n = np.arange(H)[None, :]
    out = []
    for q in (0, 1):
        ph = -2.0 * math.pi * ((n * (2 * k + q)) % N) / N
        c, s = np.cos(ph) / 16.0, np.sin(ph) / 16.0
        out.append(np.block([[c, -s], [s, c]]))
    t = np.stack(out).astype(np.float32)
    def hl(a):
        hi = a.astype(ml_dtypes.bfloat16)
        lo = (a - hi.astype(np.float32)).astype(ml_dtypes.bfloat16)
        return hi, lo
    hi, lo = hl(t)
    left = np.concatenate([hi, hi, lo], axis=2)
    hiT, loT = hi.transpose(0, 2, 1), lo.transpose(0, 2, 1)
    leftT = np.concatenate([hiT, hiT, loT], axis=2)
    right = np.concatenate([hi, hi, lo], axis=1)
    rightT = np.concatenate([hiT, hiT, loT], axis=1)
    perm = np.zeros((N, N), np.float32)
    for i in range(H):
        perm[2 * i, i] = 1; perm[2 * i + 1, H + i] = 1
    return left, leftT, right, rightT, perm.astype(ml_dtypes.bfloat16)

def dot(a, b):
    return jnp.dot(a, b, preferred_element_type=jnp.float32)

def lmul(t, x):
    hi, lo = split(x)
    return dot(t, jnp.concatenate([hi, lo, hi], axis=0))

def rmul(x, t):
    hi, lo = split(x)
    return dot(jnp.concatenate([hi, lo, hi], axis=1), t)

def compute_kernel(count_ref, off_ref, ext, probe, pat, left, leftT, right, rightT, perm,
                   gext, pgrad, loss_ref, patch, psi, res, acc, swap):
    gext[...] = jnp.zeros_like(gext)
    pgrad[...] = jnp.zeros_like(pgrad)
    loss_ref[...] = jnp.zeros_like(loss_ref)

    def slot(s, _):
        r = off_ref[2 * s]
        c = off_ref[2 * s + 1]
        ca = pl.multiple_of(c // 128 * 128, 128)
        cs = c - ca
        ra = pl.multiple_of(r // 8 * 8, 8)
        rs = r - ra
        for comp in (0, 1):
            x = ext[comp, pl.ds(ra, 264), pl.ds(ca, 384)]
            x = pltpu.roll(x, 384 - cs, 1)[:, :N]
            patch[comp] = pltpu.roll(x, 264 - rs, 0)[:N]
        hi, lo = split(pat[s])
        y = dot(hi, perm[...]) + dot(lo, perm[...])
        for q in (0, 1):
            swap[q] = y[:, q * H:(q + 1) * H]
        for q in (0, 1):
            for p in (0, 1):
                res[q, p * H:(p + 1) * H, :] = -swap[q, pl.ds(p, H, stride=2), :]

        def fwd(m, _):
            qr, qi, orr, oi = probe[0, m], probe[1, m], patch[0], patch[1]
            er = qr * orr - qi * oi
            ei = qr * oi + qi * orr
            L = []
            for p in (0, 1):
                f = (lambda a: a[:H] + a[H:]) if p == 0 else (lambda a: a[:H] - a[H:])
                L.append(lmul(left[p], jnp.concatenate([f(er), f(ei)], axis=0)))
            re = jnp.concatenate([L[0][:H], L[1][:H]], axis=0)
            im = jnp.concatenate([L[0][H:], L[1][H:]], axis=0)
            for q in (0, 1):
                f = (lambda a: a[:, :H] + a[:, H:]) if q == 0 else (lambda a: a[:, :H] - a[:, H:])
                x = rmul(jnp.concatenate([f(re), f(im)], axis=1), rightT[q])
                psi[m, q] = x
                res[q] += x[:, :H] * x[:, :H] + x[:, H:] * x[:, H:]
            return 0
        lax.fori_loop(0, 4, fwd, 0)
        loss_ref[...] += jnp.sum((res[0] * res[0] + res[1] * res[1]).reshape(32, 8, 128), axis=0)
        acc[...] = jnp.zeros_like(acc)

        def bwd(m, _):
            t = []
            for q in (0, 1):
                R = res[q]
                t.append(rmul(psi[m, q] * jnp.concatenate([R, R], axis=1), right[q]))
            x0, x1 = t[0] + t[1], t[0] - t[1]
            L = []
            for p in (0, 1):
                sl = slice(p * H, (p + 1) * H)
                y = jnp.concatenate([
                    jnp.concatenate([x0[sl, :H], x1[sl, :H]], axis=1),
                    jnp.concatenate([x0[sl, H:], x1[sl, H:]], axis=1)], axis=0)
                L.append(lmul(leftT[p], y))
            top, bot = L[0] + L[1], L[0] - L[1]
            for i, b in enumerate((top, bot)):
                sl = slice(i * H, (i + 1) * H)
                br, bi = b[:H], b[H:]
                qr, qi = probe[0, m, sl], probe[1, m, sl]
                orr, oi = patch[0, sl], patch[1, sl]
                acc[0, sl, :N] += qr * br + qi * bi
                acc[1, sl, :N] += qr * bi - qi * br
                pgrad[0, m, sl] += orr * br + oi * bi
                pgrad[1, m, sl] += orr * bi - oi * br
            return 0
        lax.fori_loop(0, 4, bwd, 0)
        for comp in (0, 1):
            x = pltpu.roll(acc[comp], rs, 0)
            gext[comp, pl.ds(ra, 264), pl.ds(ca, 384)] += pltpu.roll(x, cs, 1)
        return 0

    lax.fori_loop(0, count_ref[0], slot, 0)

def compute(count, offs, ext, probe, pat):
    left, leftT, right, rightT, perm = [jnp.asarray(t) for t in tables()]
    V = pl.BlockSpec(memory_space=pltpu.VMEM)
    S = pl.BlockSpec(memory_space=pltpu.SMEM)
    return pl.pallas_call(
        compute_kernel,
        out_shape=(jax.ShapeDtypeStruct((2, 776, 896), jnp.float32),
                   jax.ShapeDtypeStruct((2, 4, N, N), jnp.float32),
                   jax.ShapeDtypeStruct((8, 128), jnp.float32)),
        in_specs=[S, S] + [V] * 8,
        out_specs=(V, V, V),
        scratch_shapes=[pltpu.VMEM((2, N, N), jnp.float32), pltpu.VMEM((4, 2, N, N), jnp.float32),
                        pltpu.VMEM((2, N, H), jnp.float32), pltpu.VMEM((2, 264, 384), jnp.float32),
                        pltpu.VMEM((2, N, H), jnp.float32)],
        compiler_params=pltpu.CompilerParams(vmem_limit_bytes=56 << 20),
        name="compute",
    )(count, offs, ext, probe, pat, left, leftT, right, rightT, perm)


def shifted(shard, axis, by):
    size = lax.axis_size(axis)
    pairs = [(i, i + by) for i in range(size) if 0 <= i + by < size]
    return lax.ppermute(shard, axis, pairs)


def body(object_slab, probe_field, patterns, offsets, counts):
    tile = object_slab.shape[1]
    pixels = probe_field.shape[2]
    from_right = shifted(object_slab[:, :, :pixels], "col", -1)
    widened = jnp.concatenate([object_slab, from_right], axis=2)
    from_below = shifted(widened[:, :pixels, :], "row", -1)
    extended = jnp.concatenate([widened, from_below], axis=1)
    extended = jnp.pad(extended, ((0, 0), (0, 8), (0, 128)))
    device_id = lax.axis_index(("row", "col"))
    own_count = lax.dynamic_slice_in_dim(counts, device_id, 1)
    grad_ext, grad_probe, loss = compute(own_count, offsets[0].reshape(-1), extended, probe_field, patterns[0])
    from_above = shifted(grad_ext[:, tile : tile + pixels, : tile + pixels], "row", 1)
    upper = grad_ext[:, :tile, : tile + pixels].at[:, :pixels, :].add(from_above)
    from_left = shifted(upper[:, :, tile:], "col", 1)
    object_grad = upper[:, :, :tile].at[:, :, :pixels].add(from_left)
    probe_peak = jnp.max(jnp.sum(probe_field[0] * probe_field[0] + probe_field[1] * probe_field[1], axis=0))
    new_object = object_slab - object_grad / probe_peak
    local_peak = jnp.max(object_slab[0] * object_slab[0] + object_slab[1] * object_slab[1])
    largest = lax.pmax(local_peak, ("row", "col"))
    scans = jnp.sum(counts).astype(jnp.float32) * (pixels * pixels)
    probe_total, loss_total = lax.psum((grad_probe, 0.5 * jnp.sum(loss)), ("row", "col"))
    new_probe = probe_field - probe_total / largest
    return (new_object, new_probe, loss_total / scans)


def solution(mesh):
    placed = (
        P(None, "row", "col"),
        P(),
        P(("row", "col"), None, None, None),
        P(("row", "col"), None, None),
        P(),
    )
    return jax.shard_map(
        body,
        mesh=mesh,
        in_specs=placed,
        out_specs=(P(None, "row", "col"), P(), P()),
        check_vma=False,
    )
```

```python
import math

import jax
import jax.numpy as jnp
import ml_dtypes
import numpy as np
from jax import lax
from jax.experimental import pallas as pl
from jax.experimental.pallas import tpu as pltpu
from jax.sharding import PartitionSpec as P

N = 256
H = 128


def split(x):
    hi = x.astype(jnp.bfloat16)
    lo = (x - hi.astype(jnp.float32)).astype(jnp.bfloat16)
    return hi, lo

def tables():
    k = np.arange(H)[:, None]
    n = np.arange(H)[None, :]
    out = []
    for q in (0, 1):
        ph = -2.0 * math.pi * ((n * (2 * k + q)) % N) / N
        c, s = np.cos(ph) / 16.0, np.sin(ph) / 16.0
        out.append(np.block([[c, -s], [s, c]]))
    t = np.stack(out).astype(np.float32)
    def hl(a):
        hi = a.astype(ml_dtypes.bfloat16)
        lo = (a - hi.astype(np.float32)).astype(ml_dtypes.bfloat16)
        return hi, lo
    hi, lo = hl(t)
    left = np.concatenate([hi, hi, lo], axis=2)
    hiT, loT = hi.transpose(0, 2, 1), lo.transpose(0, 2, 1)
    leftT = np.concatenate([hiT, hiT, loT], axis=2)
    right = np.concatenate([hi, hi, lo], axis=1)
    rightT = np.concatenate([hiT, hiT, loT], axis=1)
    perm = np.zeros((N, N), np.float32)
    for i in range(H):
        perm[2 * i, i] = 1; perm[2 * i + 1, H + i] = 1
    return left, leftT, right, rightT, perm.astype(ml_dtypes.bfloat16)

def dot(a, b):
    return jnp.dot(a, b, preferred_element_type=jnp.float32)

def lmul(t, x):
    hi, lo = split(x)
    return dot(t, jnp.concatenate([hi, lo, hi], axis=0))

def rmul(x, t):
    hi, lo = split(x)
    return dot(jnp.concatenate([hi, lo, hi], axis=1), t)

def compute_kernel(counts, offsets, obj, hr, hb, probe, patterns, left, leftT, right, rightT, perm,
                   gext, pgrad, loss_ref, ext, patch, psi, res, acc, swap, local):
    loads = [
        pltpu.make_async_copy(obj, ext.at[:, 0 : 2 * N, 0 : 2 * N], local.at[0]),
        pltpu.make_async_copy(hr, ext.at[:, 0 : 2 * N, 2 * N : 3 * N], local.at[1]),
        pltpu.make_async_copy(hb, ext.at[:, 2 * N : 3 * N, 0 : 3 * N], local.at[2]),
    ]
    for load in loads:
        load.start()
    row = lax.axis_index("row")
    col = lax.axis_index("col")
    count = counts[row * 16 + col]
    gext[...] = jnp.zeros_like(gext)
    pgrad[...] = jnp.zeros_like(pgrad)
    loss_ref[...] = jnp.zeros_like(loss_ref)
    for load in loads:
        load.wait()

    @pl.when(col == 15)
    def _():
        ext[:, :, 2 * N : 3 * N] = jnp.zeros((2, 776, N), jnp.float32)

    @pl.when(row == 7)
    def _():
        ext[:, 2 * N : 3 * N, :] = jnp.zeros((2, N, 896), jnp.float32)

    def slot(s, _):
        r = offsets[0, s, 0]
        c = offsets[0, s, 1]
        ca = pl.multiple_of(c // 128 * 128, 128)
        cs = c - ca
        ra = pl.multiple_of(r // 8 * 8, 8)
        rs = r - ra
        for comp in (0, 1):
            x = ext[comp, pl.ds(ra, 264), pl.ds(ca, 384)]
            x = pltpu.roll(x, 384 - cs, 1)[:, :N]
            patch[comp] = pltpu.roll(x, 264 - rs, 0)[:N]
        hi, lo = split(patterns[0, s])
        y = dot(hi, perm[...]) + dot(lo, perm[...])
        for q in (0, 1):
            swap[q] = y[:, q * H:(q + 1) * H]
        for q in (0, 1):
            for p in (0, 1):
                res[q, p * H:(p + 1) * H, :] = -swap[q, pl.ds(p, H, stride=2), :]

        def fwd(m, _):
            qr, qi, orr, oi = probe[0, m], probe[1, m], patch[0], patch[1]
            er = qr * orr - qi * oi
            ei = qr * oi + qi * orr
            L = []
            for p in (0, 1):
                f = (lambda a: a[:H] + a[H:]) if p == 0 else (lambda a: a[:H] - a[H:])
                L.append(lmul(left[p], jnp.concatenate([f(er), f(ei)], axis=0)))
            re = jnp.concatenate([L[0][:H], L[1][:H]], axis=0)
            im = jnp.concatenate([L[0][H:], L[1][H:]], axis=0)
            for q in (0, 1):
                f = (lambda a: a[:, :H] + a[:, H:]) if q == 0 else (lambda a: a[:, :H] - a[:, H:])
                x = rmul(jnp.concatenate([f(re), f(im)], axis=1), rightT[q])
                psi[m, q] = x
                res[q] += x[:, :H] * x[:, :H] + x[:, H:] * x[:, H:]
            return 0
        lax.fori_loop(0, 4, fwd, 0)
        loss_ref[...] += jnp.sum((res[0] * res[0] + res[1] * res[1]).reshape(32, 8, 128), axis=0)
        acc[...] = jnp.zeros_like(acc)

        def bwd(m, _):
            t = []
            for q in (0, 1):
                R = res[q]
                t.append(rmul(psi[m, q] * jnp.concatenate([R, R], axis=1), right[q]))
            x0, x1 = t[0] + t[1], t[0] - t[1]
            L = []
            for p in (0, 1):
                sl = slice(p * H, (p + 1) * H)
                y = jnp.concatenate([
                    jnp.concatenate([x0[sl, :H], x1[sl, :H]], axis=1),
                    jnp.concatenate([x0[sl, H:], x1[sl, H:]], axis=1)], axis=0)
                L.append(lmul(leftT[p], y))
            top, bot = L[0] + L[1], L[0] - L[1]
            for i, b in enumerate((top, bot)):
                sl = slice(i * H, (i + 1) * H)
                br, bi = b[:H], b[H:]
                qr, qi = probe[0, m, sl], probe[1, m, sl]
                orr, oi = patch[0, sl], patch[1, sl]
                acc[0, sl, :N] += qr * br + qi * bi
                acc[1, sl, :N] += qr * bi - qi * br
                pgrad[0, m, sl] += orr * br + oi * bi
                pgrad[1, m, sl] += orr * bi - oi * br
            return 0
        lax.fori_loop(0, 4, bwd, 0)
        for comp in (0, 1):
            x = pltpu.roll(acc[comp], rs, 0)
            gext[comp, pl.ds(ra, 264), pl.ds(ca, 384)] += pltpu.roll(x, cs, 1)
        return 0

    lax.fori_loop(0, count, slot, 0)
    scans = lax.fori_loop(0, counts.shape[0], lambda i, t: t + counts[i], 0)
    loss_ref[...] = loss_ref[...] * (0.5 / (scans.astype(jnp.float32) * (N * N)))

    @pl.when(col == 15)
    def _():
        gext[:, :, 2 * N : 3 * N] = jnp.zeros((2, 776, N), jnp.float32)

    @pl.when(row == 7)
    def _():
        gext[:, 2 * N : 3 * N, :] = jnp.zeros((2, N, 896), jnp.float32)


def compute(counts, offsets, obj, hr, hb, probe, patterns):
    consts = [jnp.asarray(t) for t in tables()]
    V = pl.BlockSpec(memory_space=pltpu.VMEM)
    S = pl.BlockSpec(memory_space=pltpu.SMEM)
    A = pl.BlockSpec(memory_space=pl.ANY)
    return pl.pallas_call(
        compute_kernel,
        out_shape=(
            jax.ShapeDtypeStruct((2, 776, 896), jnp.float32),
            jax.ShapeDtypeStruct((2, 4, N, N), jnp.float32),
            jax.ShapeDtypeStruct((8, 128), jnp.float32),
        ),
        in_specs=[S, S] + [A] * 3 + [V] * 7,
        out_specs=(V, V, V),
        scratch_shapes=[
            pltpu.VMEM((2, 776, 896), jnp.float32),
            pltpu.VMEM((2, N, N), jnp.float32),
            pltpu.VMEM((4, 2, N, N), jnp.float32),
            pltpu.VMEM((2, N, H), jnp.float32),
            pltpu.VMEM((2, 264, 384), jnp.float32),
            pltpu.VMEM((2, N, H), jnp.float32),
            pltpu.SemaphoreType.DMA((3,)),
        ],
        compiler_params=pltpu.CompilerParams(vmem_limit_bytes=56 << 20),
        name="compute",
    )(counts, offsets, obj, hr, hb, probe, patterns, *consts)


MESH = pl.DeviceIdType.MESH
F32 = jnp.float32


def place():
    row = lax.axis_index("row")
    col = lax.axis_index("col")
    return col // 4, row // 2, col % 4, row % 2


def device_at(x, y, z, k):
    return (lax.rem(y + 8, 4) * 2 + k, lax.rem(x + 8, 4) * 4 + lax.rem(z + 8, 4))


def neighbours():
    row = lax.axis_index("row")
    col = lax.axis_index("col")
    left = (row, lax.rem(col + 15, 16))
    right = (row, lax.rem(col + 1, 16))
    above = (lax.rem(row + 7, 8), col)
    below = (lax.rem(row + 1, 8), col)
    return left, right, above, below


def groups():
    x, y, z, k = place()
    return {
        "k": [device_at(x, y, z, 1 - k)],
        "x": [device_at(x + d, y, z, k) for d in (1, 2, 3)],
        "y": [device_at(x, y + d, z, k) for d in (1, 2, 3)],
        "z": [device_at(x, y, z + d, k) for d in (1, 2, 3)],
    }


def greet():
    peers = list(neighbours())
    for axis in ("k", "x", "y", "z"):
        peers += groups()[axis]
    barrier = pltpu.get_barrier_semaphore()
    for peer in peers:
        pl.semaphore_signal(barrier, inc=1, device_id=peer, device_id_type=MESH)
    pl.semaphore_wait(barrier, len(peers))


def remote(src, dst, send, recv, i, peer):
    copy = pltpu.make_async_remote_copy(
        src_ref=src, dst_ref=dst, send_sem=send.at[i], recv_sem=recv.at[i], device_id=peer, device_id_type=MESH
    )
    copy.start()
    return copy


class Small:
    def __init__(self, op, value, slots, send, recv, base):
        self.op, self.value, self.slots, self.send, self.recv, self.base = op, value, slots, send, recv, base
        self.step, self.at = 0, 0

    def start(self):
        peers = groups()["kxyz"[self.step]]
        self.copies = []
        for peer in peers:
            self.copies.append(
                remote(self.value.at[self.step], self.slots.at[self.at], self.send, self.recv, self.base + self.at, peer)
            )
            self.at += 1

    def finish(self):
        total = self.value[self.step]
        first = self.at - len(self.copies)
        for i, copy in enumerate(self.copies):
            copy.wait()
            total = self.op(total, self.slots[first + i])
        self.step += 1
        self.value[self.step] = total


def halo_kernel(obj, hr, hb, peak, mine, value, slots, local, send, recv):
    own = pltpu.make_async_copy(obj, mine, local.at[0])
    own.start()
    left, right, above, below = neighbours()
    greet()
    n = 256
    top = remote(obj.at[:, 0:n, 0:n], hr.at[:, 0:n, :], send, recv, 0, left)
    side = remote(obj.at[:, 0:n, :], hb.at[:, :, 0 : 2 * n], send, recv, 2, above)
    bottom = remote(obj.at[:, n : 2 * n, 0:n], hr.at[:, n : 2 * n, :], send, recv, 1, left)
    own.wait()

    def largest(i, best):
        re = mine[0, pl.ds(pl.multiple_of(i * 16, 16), 16), :]
        im = mine[1, pl.ds(pl.multiple_of(i * 16, 16), 16), :]
        return jnp.maximum(best, re * re + im * im)

    best = lax.fori_loop(0, 32, largest, jnp.zeros((16, 512), F32))
    value[0] = jnp.full((8, 128), jnp.max(best), F32)
    peaks = Small(jnp.maximum, value, slots, send, recv, 4)
    for _ in range(4):
        peaks.start()
        peaks.finish()
    peak[...] = value[4]
    top.wait_recv()
    corner = remote(hr.at[:, 0:n, :], hb.at[:, :, 2 * n : 3 * n], send, recv, 3, above)
    top.wait_send()
    side.wait()
    corner.wait()
    bottom.wait()


def halo(obj):
    V = pl.BlockSpec(memory_space=pltpu.VMEM)
    A = pl.BlockSpec(memory_space=pl.ANY)
    return pl.pallas_call(
        halo_kernel,
        out_shape=(
            jax.ShapeDtypeStruct((2, 512, 256), F32),
            jax.ShapeDtypeStruct((2, 256, 768), F32),
            jax.ShapeDtypeStruct((8, 128), F32),
        ),
        in_specs=[A],
        out_specs=(A, A, V),
        scratch_shapes=[
            pltpu.VMEM((2, 512, 512), F32),
            pltpu.VMEM((5, 8, 128), F32),
            pltpu.VMEM((10, 8, 128), F32),
            pltpu.SemaphoreType.DMA((1,)),
            pltpu.SemaphoreType.DMA((14,)),
            pltpu.SemaphoreType.DMA((14,)),
        ],
        compiler_params=pltpu.CompilerParams(collective_id=0, has_side_effects=True, vmem_limit_bytes=32 << 20),
        name="halo",
    )(obj)


def shares(axis, rows):
    x, y, z, k = place()
    mine = {"k": k, "x": x, "y": y, "z": z}[axis]
    size = 2 if axis == "k" else 4
    part = rows // size
    others = [(lax.rem(mine + d, size) * part) for d in range(1, size)]
    return mine * part, others, part


def exchange_kernel(gext, pg, obj, probe, peak, loss, new_obj, new_probe, loss_mean,
                    own, tile, field, total, corner, strip, over, side,
                    r0, rx, ry, rz, value, slots, local, send, recv):
    n = 256
    left, right, above, below = neighbours()
    loads = [
        pltpu.make_async_copy(pg, total, local.at[0]),
        pltpu.make_async_copy(gext.at[:, 0:n, 2 * n : 3 * n], strip, local.at[1]),
        pltpu.make_async_copy(gext.at[:, 0 : 2 * n, 0 : 2 * n], own, local.at[2]),
        pltpu.make_async_copy(obj, tile, local.at[3]),
        pltpu.make_async_copy(probe, field, local.at[4]),
    ]
    for load in loads:
        load.start()
    greet()
    t1 = remote(gext.at[:, 2 * n : 3 * n, 2 * n : 3 * n], corner, send, recv, 0, below)
    t2 = remote(gext.at[:, n : 2 * n, 2 * n : 3 * n], side.at[:, n : 2 * n, :], send, recv, 1, right)
    t3 = remote(gext.at[:, 2 * n : 3 * n, 0 : 2 * n], over, send, recv, 2, below)
    value[0] = loss[...]
    misfit = Small(jnp.add, value, slots, send, recv, 4)
    misfit.start()
    group = groups()
    at = 14
    base, rows = 0, 2048
    trail = []
    pending = []
    for axis, got in (("k", r0), ("x", rx), ("y", ry), ("z", rz)):
        mine, others, part = shares(axis, rows)
        copies = []
        source = pg if axis == "k" else total
        for i, (peer, other) in enumerate(zip(group[axis], others)):
            copies.append(remote(source.at[pl.ds(pl.multiple_of(base + other, 16), part), :], got.at[i], send, recv, at, peer))
            at += 1
        if axis == "k":
            for load in loads:
                load.wait()
        misfit.finish()
        if axis != "z":
            misfit.start()
        if axis == "x":
            t1.wait_recv()
            strip[...] += corner[...]
            t4 = remote(strip, side.at[:, 0:n, :], send, recv, 3, right)
        keep = pl.ds(pl.multiple_of(base + mine, 16), part)
        for i, copy in enumerate(copies):
            copy.wait_recv()
        pending += copies
        sums = total[keep, :]
        for i in range(len(copies)):
            sums += got[i]
        total[keep, :] = sums
        trail.append((axis, base, rows, keep))
        base, rows = base + mine, part
    loss_mean[0, 0] = jnp.sum(value[4])
    keep = pl.ds(pl.multiple_of(base, 16), rows)
    scale = 1.0 / peak[0:1, 0:1]
    new_probe[keep, :] = field[keep, :] - total[keep, :] * scale
    for axis, base, rows, keep in reversed(trail):
        whole = pl.ds(pl.multiple_of(base, 16), rows)
        mine, others, part = shares(axis, rows)
        copies = []
        for peer in group[axis]:
            copies.append(remote(new_probe.at[keep, :], new_probe.at[keep, :], send, recv, at, peer))
            at += 1
        for copy in copies:
            copy.wait_recv()
        pending += copies
    probe_peak = jnp.max(
        sum(field[m * n : (m + 1) * n, :] * field[m * n : (m + 1) * n, :] for m in range(8))
    )
    inverse = 1.0 / probe_peak
    t3.wait_recv()
    own[:, 0:n, :] += over[...]
    new_obj[:, :, n : 2 * n] = tile[:, :, n : 2 * n] - own[:, :, n : 2 * n] * inverse
    t2.wait_recv()
    t4.wait_recv()
    new_obj[:, :, 0:n] = tile[:, :, 0:n] - (own[:, :, 0:n] + side[...]) * inverse
    for copy in pending + [t1, t2, t3, t4]:
        copy.wait_send()


def exchange(gext, pg, obj, probe, peak, loss):
    V = pl.BlockSpec(memory_space=pltpu.VMEM)
    A = pl.BlockSpec(memory_space=pl.ANY)
    S = pl.BlockSpec(memory_space=pltpu.SMEM)
    copies = 14 + 2 * 10
    new_obj, new_probe, loss_mean = pl.pallas_call(
        exchange_kernel,
        out_shape=(
            jax.ShapeDtypeStruct((2, 512, 512), F32),
            jax.ShapeDtypeStruct((2048, 256), F32),
            jax.ShapeDtypeStruct((1, 1), F32),
        ),
        in_specs=[A, A, A, A, V, V],
        out_specs=(V, V, S),
        scratch_shapes=[
            pltpu.VMEM((2, 512, 512), F32),
            pltpu.VMEM((2, 512, 512), F32),
            pltpu.VMEM((2048, 256), F32),
            pltpu.VMEM((2048, 256), F32),
            pltpu.VMEM((2, 256, 256), F32),
            pltpu.VMEM((2, 256, 256), F32),
            pltpu.VMEM((2, 256, 512), F32),
            pltpu.VMEM((2, 512, 256), F32),
            pltpu.VMEM((1, 1024, 256), F32),
            pltpu.VMEM((3, 256, 256), F32),
            pltpu.VMEM((3, 64, 256), F32),
            pltpu.VMEM((3, 16, 256), F32),
            pltpu.VMEM((5, 8, 128), F32),
            pltpu.VMEM((10, 8, 128), F32),
            pltpu.SemaphoreType.DMA((5,)),
            pltpu.SemaphoreType.DMA((copies,)),
            pltpu.SemaphoreType.DMA((copies,)),
        ],
        compiler_params=pltpu.CompilerParams(collective_id=1, has_side_effects=True, vmem_limit_bytes=48 << 20),
        name="exchange",
    )(gext, pg.reshape(2048, 256), obj, probe.reshape(2048, 256), peak, loss)
    return new_obj, new_probe.reshape(probe.shape), loss_mean.reshape(())


def body(object_slab, probe_field, patterns, offsets, counts):
    hr, hb, peak = halo(object_slab)
    gext, pg, loss = compute(counts, offsets, object_slab, hr, hb, probe_field, patterns)
    return exchange(gext, pg, object_slab, probe_field, peak, loss)


def solution(mesh):
    placed = (
        P(None, "row", "col"),
        P(),
        P(("row", "col"), None, None, None),
        P(("row", "col"), None, None),
        P(),
    )
    return jax.shard_map(
        body,
        mesh=mesh,
        in_specs=placed,
        out_specs=(P(None, "row", "col"), P(), P()),
        check_vma=False,
    )
```

```python
import math

import jax
import jax.numpy as jnp
import ml_dtypes
import numpy as np
from jax import lax
from jax.experimental import pallas as pl
from jax.experimental.pallas import tpu as pltpu
from jax.sharding import PartitionSpec as P

N = 256
H = 128


def split(x):
    hi = x.astype(jnp.bfloat16)
    lo = (x - hi.astype(jnp.float32)).astype(jnp.bfloat16)
    return hi, lo

def tables():
    k = np.arange(H)[:, None]
    n = np.arange(H)[None, :]
    out = []
    for q in (0, 1):
        ph = -2.0 * math.pi * ((n * (2 * k + q)) % N) / N
        c, s = np.cos(ph) / 16.0, np.sin(ph) / 16.0
        out.append(np.block([[c, -s], [s, c]]))
    t = np.stack(out).astype(np.float32)
    def hl(a):
        hi = a.astype(ml_dtypes.bfloat16)
        lo = (a - hi.astype(np.float32)).astype(ml_dtypes.bfloat16)
        return hi, lo
    hi, lo = hl(t)
    left = np.concatenate([hi, hi, lo], axis=2)
    hiT, loT = hi.transpose(0, 2, 1), lo.transpose(0, 2, 1)
    leftT = np.concatenate([hiT, hiT, loT], axis=2)
    right = np.concatenate([hi, hi, lo], axis=1)
    rightT = np.concatenate([hiT, hiT, loT], axis=1)
    perm = np.zeros((N, N), np.float32)
    for i in range(H):
        perm[2 * i, i] = 1; perm[2 * i + 1, H + i] = 1
    return left, leftT, right, rightT, perm.astype(ml_dtypes.bfloat16)

def dot(a, b):
    return jnp.dot(a, b, preferred_element_type=jnp.float32)

def lmul(t, x):
    hi, lo = split(x)
    return dot(t, jnp.concatenate([hi, lo, hi], axis=0))

def rmul(x, t):
    hi, lo = split(x)
    return dot(jnp.concatenate([hi, lo, hi], axis=1), t)

def compute_kernel(counts, offsets, obj, hr, hb, probe, patterns, left, leftT, right, rightT, perm,
                   gext, pgrad, loss_ref, ext, patch, psi, res, acc, swap, local):
    loads = [
        pltpu.make_async_copy(obj, ext.at[:, 0 : 2 * N, 0 : 2 * N], local.at[0]),
        pltpu.make_async_copy(hr, ext.at[:, 0 : 2 * N, 2 * N : 3 * N], local.at[1]),
        pltpu.make_async_copy(hb, ext.at[:, 2 * N : 3 * N, 0 : 3 * N], local.at[2]),
    ]
    for load in loads:
        load.start()
    row = lax.axis_index("row")
    col = lax.axis_index("col")
    count = counts[row * 16 + col]
    gext[...] = jnp.zeros_like(gext)
    pgrad[...] = jnp.zeros_like(pgrad)
    loss_ref[...] = jnp.zeros_like(loss_ref)
    for load in loads:
        load.wait()

    @pl.when(col == 15)
    def _():
        ext[:, :, 2 * N : 3 * N] = jnp.zeros((2, 776, N), jnp.float32)

    @pl.when(row == 7)
    def _():
        ext[:, 2 * N : 3 * N, :] = jnp.zeros((2, N, 896), jnp.float32)

    def slot(s, _):
        r = offsets[0, s, 0]
        c = offsets[0, s, 1]
        ca = pl.multiple_of(c // 128 * 128, 128)
        cs = c - ca
        ra = pl.multiple_of(r // 8 * 8, 8)
        rs = r - ra
        for comp in (0, 1):
            x = ext[comp, pl.ds(ra, 264), pl.ds(ca, 384)]
            x = pltpu.roll(x, 384 - cs, 1)[:, :N]
            patch[comp] = pltpu.roll(x, 264 - rs, 0)[:N]
        hi, lo = split(patterns[0, s])
        y = dot(hi, perm[...]) + dot(lo, perm[...])
        for q in (0, 1):
            swap[q] = y[:, q * H:(q + 1) * H]
        for q in (0, 1):
            for p in (0, 1):
                res[q, p * H:(p + 1) * H, :] = -swap[q, pl.ds(p, H, stride=2), :]

        def fwd(m, _):
            qr, qi, orr, oi = probe[0, m], probe[1, m], patch[0], patch[1]
            er = qr * orr - qi * oi
            ei = qr * oi + qi * orr
            L = []
            for p in (0, 1):
                f = (lambda a: a[:H] + a[H:]) if p == 0 else (lambda a: a[:H] - a[H:])
                L.append(lmul(left[p], jnp.concatenate([f(er), f(ei)], axis=0)))
            re = jnp.concatenate([L[0][:H], L[1][:H]], axis=0)
            im = jnp.concatenate([L[0][H:], L[1][H:]], axis=0)
            for q in (0, 1):
                f = (lambda a: a[:, :H] + a[:, H:]) if q == 0 else (lambda a: a[:, :H] - a[:, H:])
                x = rmul(jnp.concatenate([f(re), f(im)], axis=1), rightT[q])
                psi[m, q] = x
                res[q] += x[:, :H] * x[:, :H] + x[:, H:] * x[:, H:]
            return 0
        lax.fori_loop(0, 4, fwd, 0, unroll=True)
        loss_ref[...] += jnp.sum((res[0] * res[0] + res[1] * res[1]).reshape(32, 8, 128), axis=0)
        acc[...] = jnp.zeros_like(acc)

        def bwd(m, _):
            t = []
            for q in (0, 1):
                R = res[q]
                t.append(rmul(psi[m, q] * jnp.concatenate([R, R], axis=1), right[q]))
            x0, x1 = t[0] + t[1], t[0] - t[1]
            L = []
            for p in (0, 1):
                sl = slice(p * H, (p + 1) * H)
                y = jnp.concatenate([
                    jnp.concatenate([x0[sl, :H], x1[sl, :H]], axis=1),
                    jnp.concatenate([x0[sl, H:], x1[sl, H:]], axis=1)], axis=0)
                L.append(lmul(leftT[p], y))
            top, bot = L[0] + L[1], L[0] - L[1]
            for i, b in enumerate((top, bot)):
                sl = slice(i * H, (i + 1) * H)
                br, bi = b[:H], b[H:]
                qr, qi = probe[0, m, sl], probe[1, m, sl]
                orr, oi = patch[0, sl], patch[1, sl]
                acc[0, sl, :N] += qr * br + qi * bi
                acc[1, sl, :N] += qr * bi - qi * br
                pgrad[0, m, sl] += orr * br + oi * bi
                pgrad[1, m, sl] += orr * bi - oi * br
            return 0
        lax.fori_loop(0, 4, bwd, 0, unroll=True)
        for comp in (0, 1):
            x = pltpu.roll(acc[comp], rs, 0)
            gext[comp, pl.ds(ra, 264), pl.ds(ca, 384)] += pltpu.roll(x, cs, 1)
        return 0

    lax.fori_loop(0, count, slot, 0)
    scans = lax.fori_loop(0, counts.shape[0], lambda i, t: t + counts[i], 0)
    loss_ref[...] = loss_ref[...] * (0.5 / (scans.astype(jnp.float32) * (N * N)))

    @pl.when(col == 15)
    def _():
        gext[:, :, 2 * N : 3 * N] = jnp.zeros((2, 776, N), jnp.float32)

    @pl.when(row == 7)
    def _():
        gext[:, 2 * N : 3 * N, :] = jnp.zeros((2, N, 896), jnp.float32)


def compute(counts, offsets, obj, hr, hb, probe, patterns):
    consts = [jnp.asarray(t) for t in tables()]
    V = pl.BlockSpec(memory_space=pltpu.VMEM)
    S = pl.BlockSpec(memory_space=pltpu.SMEM)
    A = pl.BlockSpec(memory_space=pl.ANY)
    return pl.pallas_call(
        compute_kernel,
        out_shape=(
            jax.ShapeDtypeStruct((2, 776, 896), jnp.float32),
            jax.ShapeDtypeStruct((2, 4, N, N), jnp.float32),
            jax.ShapeDtypeStruct((8, 128), jnp.float32),
        ),
        in_specs=[S, S] + [A] * 3 + [V] * 7,
        out_specs=(V, V, V),
        scratch_shapes=[
            pltpu.VMEM((2, 776, 896), jnp.float32),
            pltpu.VMEM((2, N, N), jnp.float32),
            pltpu.VMEM((4, 2, N, N), jnp.float32),
            pltpu.VMEM((2, N, H), jnp.float32),
            pltpu.VMEM((2, 264, 384), jnp.float32),
            pltpu.VMEM((2, N, H), jnp.float32),
            pltpu.SemaphoreType.DMA((3,)),
        ],
        compiler_params=pltpu.CompilerParams(vmem_limit_bytes=24 << 20),
        name="compute",
    )(counts, offsets, obj, hr, hb, probe, patterns, *consts)


MESH = pl.DeviceIdType.MESH
F32 = jnp.float32


def place():
    row = lax.axis_index("row")
    col = lax.axis_index("col")
    return col // 4, row // 2, col % 4, row % 2


def device_at(x, y, z, k):
    return (lax.rem(y + 8, 4) * 2 + k, lax.rem(x + 8, 4) * 4 + lax.rem(z + 8, 4))


def neighbours():
    row = lax.axis_index("row")
    col = lax.axis_index("col")
    left = (row, lax.rem(col + 15, 16))
    right = (row, lax.rem(col + 1, 16))
    above = (lax.rem(row + 7, 8), col)
    below = (lax.rem(row + 1, 8), col)
    return left, right, above, below


def groups():
    x, y, z, k = place()
    return {
        "k": [device_at(x, y, z, 1 - k)],
        "x": [device_at(x + d, y, z, k) for d in (1, 2, 3)],
        "y": [device_at(x, y + d, z, k) for d in (1, 2, 3)],
        "z": [device_at(x, y, z + d, k) for d in (1, 2, 3)],
    }


def greet(peers):
    barrier = pltpu.get_barrier_semaphore()
    for peer in peers:
        pl.semaphore_signal(barrier, inc=1, device_id=peer, device_id_type=MESH)
    pl.semaphore_wait(barrier, len(peers))


def remote(src, dst, send, recv, i, peer):
    copy = pltpu.make_async_remote_copy(
        src_ref=src, dst_ref=dst, send_sem=send.at[i], recv_sem=recv.at[i], device_id=peer, device_id_type=MESH
    )
    copy.start()
    return copy


class Small:
    def __init__(self, op, value, slots, send, recv, base):
        self.op, self.value, self.slots, self.send, self.recv, self.base = op, value, slots, send, recv, base
        self.step, self.at = 0, 0
        self.done = []

    def start(self):
        axis = "kxyz"[self.step]
        mine = dict(zip("xyzk", place()))[axis]
        self.slots[self.step, mine] = self.value[self.step]
        self.copies = []
        for peer in groups()[axis]:
            self.copies.append(
                remote(
                    self.value.at[self.step], self.slots.at[self.step, mine], self.send, self.recv,
                    self.base + self.at, peer,
                )
            )
            self.at += 1

    def finish(self):
        for copy in self.copies:
            copy.wait_recv()
        self.done += self.copies
        total = self.slots[self.step, 0]
        for i in range(1, len(self.copies) + 1):
            total = self.op(total, self.slots[self.step, i])
        self.step += 1
        self.value[self.step] = total


def halo_kernel(obj, hr, hb, peak, mine, local, send, recv):
    own = pltpu.make_async_copy(obj, mine, local.at[0])
    own.start()
    left, right, above, below = neighbours()
    greet(list(neighbours()))
    n = 256
    top = remote(obj.at[:, 0:n, 0:n], hr.at[:, 0:n, :], send, recv, 0, left)
    side = remote(obj.at[:, 0:n, :], hb.at[:, :, 0 : 2 * n], send, recv, 2, above)
    bottom = remote(obj.at[:, n : 2 * n, 0:n], hr.at[:, n : 2 * n, :], send, recv, 1, left)
    own.wait()

    def largest(i, best):
        re = mine[0, pl.ds(pl.multiple_of(i * 16, 16), 16), :]
        im = mine[1, pl.ds(pl.multiple_of(i * 16, 16), 16), :]
        return jnp.maximum(best, re * re + im * im)

    best = lax.fori_loop(0, 32, largest, jnp.zeros((16, 512), F32))
    peak[...] = jnp.full((8, 128), jnp.max(best), F32)
    top.wait_recv()
    corner = remote(hr.at[:, 0:n, :], hb.at[:, :, 2 * n : 3 * n], send, recv, 3, above)
    top.wait_send()
    side.wait()
    corner.wait()
    bottom.wait()


def halo(obj):
    V = pl.BlockSpec(memory_space=pltpu.VMEM)
    A = pl.BlockSpec(memory_space=pl.ANY)
    return pl.pallas_call(
        halo_kernel,
        out_shape=(
            jax.ShapeDtypeStruct((2, 512, 256), F32),
            jax.ShapeDtypeStruct((2, 256, 768), F32),
            jax.ShapeDtypeStruct((8, 128), F32),
        ),
        in_specs=[pl.BlockSpec(memory_space=pltpu.HBM)],
        out_specs=(A, A, V),
        scratch_shapes=[
            pltpu.VMEM((2, 512, 512), F32),
            pltpu.SemaphoreType.DMA((1,)),
            pltpu.SemaphoreType.DMA((4,)),
            pltpu.SemaphoreType.DMA((4,)),
        ],
        compiler_params=pltpu.CompilerParams(collective_id=0, has_side_effects=True, vmem_limit_bytes=6 << 20),
        name="halo",
    )(obj)


PARTS = ((0, 384, "xyz"), (384, 384, "yzx"), (768, 256, "zxy"))


def exchange_kernel(gext, pg, obj, probe, peak, loss, new_obj, new_probe, loss_mean,
                    strip, corner, over, side, r0, r1, r2, rz, value, slots, send, recv):
    n = 256
    left, right, above, below = neighbours()
    group = groups()
    x, y, z, k = place()
    index = {"x": x, "y": y, "z": z, "k": k}
    counter = [0]

    def push(src, dst, peer):
        counter[0] += 1
        return remote(src, dst, send, recv, counter[0] - 1, peer)

    def rows(start, size):
        return pl.ds(pl.multiple_of(start, 8), size)

    def op(a, b):
        first = lax.broadcasted_iota(jnp.int32, (16, 128), 0) < 8
        return jnp.where(first, a + b, jnp.maximum(a, b))

    everyone = [group[a][i] for a in "kxyz" for i in range(len(group[a]))] + [left, right, above, below]
    greet(everyone)
    sent = []
    over_sent, side_sent, corner_sent = [], [], []

    def push_corner(i):
        m = pl.ds(2 * n + 128 * i, 128)
        corner_sent.append(push(gext.at[:, m, 2 * n : 3 * n], corner.at[:, 128 * i : 128 * i + 128], below))

    def push_over(i):
        m = pl.ds(2 * n + 64 * i, 64)
        over_sent.append(push(gext.at[:, m, 0 : 2 * n], over.at[:, 64 * i : 64 * i + 64], below))

    def push_side(i):
        if i < 4:
            m = pl.ds(n + 64 * i, 64)
            side_sent.append(push(gext.at[:, m, 2 * n : 3 * n], side.at[:, m], right))
        else:
            m = pl.ds(64 * i - n, 64)
            side_sent.append(push(strip.at[:, m], side.at[:, m], right))

    def fold_corner(i):
        corner_sent[i].wait_recv()
        m = pl.ds(128 * i, 128)
        strip[:, m] = gext[:, m, 2 * n : 3 * n] + corner[:, m]

    swap = []
    for first, size, _ in PARTS:
        swap.append(push(pg.at[rows((1 - k) * 1024 + first, size)], r0.at[first : first + size], group["k"][0]))
    push_corner(0)
    push_side(0)
    value[0, 0:8] = loss[...]
    value[0, 8:16] = peak[...]
    small = Small(op, value, slots, send, recv, 84)
    small.start()

    steps = []
    for p, (first, size, axes) in enumerate(PARTS):
        swap[p].wait_recv()
        r0[first : first + size] += pg[rows(k * 1024 + first, size)]
        q = size // 4
        a = axes[0]
        copies = []
        for d, peer in enumerate(group[a]):
            other = lax.rem(index[a] + d + 1, 4)
            copies.append(push(r0.at[rows(first + other * q, q)], r1.at[d, first // 4 : first // 4 + q], peer))
        steps.append(copies)
    small.finish()
    small.start()
    push_corner(1)
    push_side(1)
    second = []
    for p, (first, size, axes) in enumerate(PARTS):
        q, e = size // 4, size // 16
        a, b, c = axes
        f1, f2 = first // 4, first // 16
        for copy in steps[p]:
            copy.wait_recv()
        sent += steps[p]
        mine = rows(first + index[a] * q, q)
        r0[mine] += r1[0, f1 : f1 + q] + r1[1, f1 : f1 + q] + r1[2, f1 : f1 + q]
        copies = []
        for d, peer in enumerate(group[b]):
            other = lax.rem(index[b] + d + 1, 4)
            copies.append(push(r0.at[rows(first + index[a] * q + other * e, e)], r2.at[d, f2 : f2 + e], peer))
        second.append(copies)
    small.finish()
    small.start()
    push_over(0)
    push_side(2)
    third = []
    for p, (first, size, axes) in enumerate(PARTS):
        q, e = size // 4, size // 16
        a, b, c = axes
        f2 = first // 16
        for copy in second[p]:
            copy.wait_recv()
        sent += second[p]
        mine = rows(first + index[a] * q + index[b] * e, e)
        total = r0[mine] + r2[0, f2 : f2 + e] + r2[1, f2 : f2 + e] + r2[2, f2 : f2 + e]
        r0[mine] = total
        rz[index[c], f2 : f2 + e] = total
        third.append([push(r0.at[mine], rz.at[index[c], f2 : f2 + e], peer) for peer in group[c]])
    small.finish()
    small.start()
    push_over(1)
    push_side(3)
    fold_corner(0)
    fold_corner(1)
    small.finish()
    loss_mean[0, 0] = jnp.sum(value[4, 0:8])
    scale = 1.0 / value[4, 8:9, 0:1]

    back = []
    for p, (first, size, axes) in enumerate(PARTS):
        q, e = size // 4, size // 16
        a, b, c = axes
        f2 = first // 16
        for copy in third[p]:
            copy.wait_recv()
        sent += third[p]
        mine = rows(k * 1024 + first + index[a] * q + index[b] * e, e)
        total = ((rz[0, f2 : f2 + e] + rz[1, f2 : f2 + e]) + rz[2, f2 : f2 + e]) + rz[3, f2 : f2 + e]
        new_probe[mine] = probe[mine] - total * scale
        back.append([push(new_probe.at[mine], new_probe.at[mine], peer) for peer in group[b]])
    push_over(2)
    push_side(4)
    last = []
    for p, (first, size, axes) in enumerate(PARTS):
        q = size // 4
        a, b, c = axes
        for copy in back[p]:
            copy.wait_recv()
        sent += back[p]
        mine = rows(k * 1024 + first + index[a] * q, q)
        last.append([push(new_probe.at[mine], new_probe.at[mine], peer) for peer in group[a]])
    push_over(3)
    for i in (5, 6, 7):
        push_side(i)
    probe_peak = jnp.max(sum(probe[m * n : (m + 1) * n] * probe[m * n : (m + 1) * n] for m in range(8)))
    inverse = 1.0 / probe_peak
    new_obj[:, n : 2 * n, n : 2 * n] = obj[:, n : 2 * n, n : 2 * n] - gext[:, n : 2 * n, n : 2 * n] * inverse
    final = []
    for p, (first, size, axes) in enumerate(PARTS):
        for copy in last[p]:
            copy.wait_recv()
        sent += last[p]
        mine = rows(k * 1024 + first, size)
        final.append(push(new_probe.at[mine], new_probe.at[mine], group["k"][0]))
    for copy in over_sent:
        copy.wait_recv()
    new_obj[:, 0:n, n : 2 * n] = obj[:, 0:n, n : 2 * n] - (gext[:, 0:n, n : 2 * n] + over[:, :, n : 2 * n]) * inverse
    for copy in side_sent:
        copy.wait_recv()
    sent += over_sent + side_sent + corner_sent + swap + final + small.done
    new_obj[:, 0:n, 0:n] = obj[:, 0:n, 0:n] - (gext[:, 0:n, 0:n] + over[:, :, 0:n] + side[:, 0:n]) * inverse
    new_obj[:, n : 2 * n, 0:n] = obj[:, n : 2 * n, 0:n] - (gext[:, n : 2 * n, 0:n] + side[:, n : 2 * n]) * inverse
    for copy in final:
        copy.wait_recv()
    for copy in sent:
        copy.wait_send()


def exchange(gext, pg, obj, probe, peak, loss):
    V = pl.BlockSpec(memory_space=pltpu.VMEM)
    S = pl.BlockSpec(memory_space=pltpu.SMEM)
    new_obj, new_probe, loss_mean = pl.pallas_call(
        exchange_kernel,
        out_shape=(
            jax.ShapeDtypeStruct((2, 512, 512), F32),
            jax.ShapeDtypeStruct((2048, 256), F32),
            jax.ShapeDtypeStruct((1, 1), F32),
        ),
        in_specs=[V] * 6,
        out_specs=(V, V, S),
        scratch_shapes=[
            pltpu.VMEM((2, 256, 256), F32),
            pltpu.VMEM((2, 256, 256), F32),
            pltpu.VMEM((2, 256, 512), F32),
            pltpu.VMEM((2, 512, 256), F32),
            pltpu.VMEM((1024, 256), F32),
            pltpu.VMEM((3, 256, 256), F32),
            pltpu.VMEM((3, 64, 256), F32),
            pltpu.VMEM((4, 64, 256), F32),
            pltpu.VMEM((5, 16, 128), F32),
            pltpu.VMEM((4, 4, 16, 128), F32),
            pltpu.SemaphoreType.DMA((96,)),
            pltpu.SemaphoreType.DMA((96,)),
        ],
        compiler_params=pltpu.CompilerParams(collective_id=1, has_side_effects=True, vmem_limit_bytes=30 << 20),
        name="exchange",
    )(gext, pg.reshape(2048, 256), obj, probe.reshape(2048, 256), peak, loss)
    return new_obj, new_probe.reshape(probe.shape), loss_mean.reshape(())


def body(object_slab, probe_field, patterns, offsets, counts):
    hr, hb, peak = halo(object_slab)
    gext, pg, loss = compute(counts, offsets, object_slab, hr, hb, probe_field, patterns)
    return exchange(gext, pg, object_slab, probe_field, peak, loss)


def solution(mesh):
    placed = (
        P(None, "row", "col"),
        P(),
        P(("row", "col"), None, None, None),
        P(("row", "col"), None, None),
        P(),
    )
    return jax.shard_map(
        body,
        mesh=mesh,
        in_specs=placed,
        out_specs=(P(None, "row", "col"), P(), P()),
        check_vma=False,
    )
```

```python
import math

import jax
import jax.numpy as jnp
import ml_dtypes
import numpy as np
from jax import lax
from jax.experimental import pallas as pl
from jax.experimental.pallas import tpu as pltpu
from jax.sharding import PartitionSpec as P

N = 256
H = 128


def split(x):
    hi = x.astype(jnp.bfloat16)
    lo = (x - hi.astype(jnp.float32)).astype(jnp.bfloat16)
    return hi, lo

def tables():
    k = np.arange(H)[:, None]
    n = np.arange(H)[None, :]
    out = []
    for q in (0, 1):
        ph = -2.0 * math.pi * ((n * (2 * k + q)) % N) / N
        c, s = np.cos(ph) / 16.0, np.sin(ph) / 16.0
        out.append(np.block([[c, -s], [s, c]]))
    t = np.stack(out).astype(np.float32)
    def hl(a):
        hi = a.astype(ml_dtypes.bfloat16)
        lo = (a - hi.astype(np.float32)).astype(ml_dtypes.bfloat16)
        return hi, lo
    hi, lo = hl(t)
    left = np.concatenate([hi, hi, lo], axis=2)
    hiT, loT = hi.transpose(0, 2, 1), lo.transpose(0, 2, 1)
    leftT = np.concatenate([hiT, hiT, loT], axis=2)
    right = np.concatenate([hi, hi, lo], axis=1)
    rightT = np.concatenate([hiT, hiT, loT], axis=1)
    perm = np.zeros((N, N), np.float32)
    for i in range(H):
        perm[2 * i, i] = 1; perm[2 * i + 1, H + i] = 1
    return left, leftT, right, rightT, perm.astype(ml_dtypes.bfloat16)

def dot(a, b):
    return jnp.dot(a, b, preferred_element_type=jnp.float32)

def lmul(t, x):
    hi, lo = split(x)
    return dot(t, jnp.concatenate([hi, lo, hi], axis=0))

def rmul(x, t):
    hi, lo = split(x)
    return dot(jnp.concatenate([hi, lo, hi], axis=1), t)

def twice(a, axis):
    return jnp.concatenate([a, lax.slice_in_dim(a, 0, N, axis=axis)], axis=axis)


def compute_kernel(counts, offsets, ext, probe, pats, left, leftT, right, rightT,
                   gext, pgrad, loss_ref, patch, psi, res, acc, xa, xb, xc, xd):
    row = lax.axis_index("row")
    col = lax.axis_index("col")
    count = counts[row * 16 + col]
    gext[...] = jnp.zeros_like(gext)
    pgrad[...] = jnp.zeros_like(pgrad)
    loss_ref[...] = jnp.zeros_like(loss_ref)

    def slot(s, _):
        r = offsets[0, 0, s]
        c = offsets[0, 1, s]
        ca = pl.multiple_of(c // 128 * 128, 128)
        cs = c - ca
        ra = pl.multiple_of(r // 8 * 8, 8)
        rs = r - ra
        sub = lax.broadcasted_iota(jnp.int32, (1, 8, N), 1)
        for comp in (0, 1):
            x = ext[comp, pl.ds(ra, 264), pl.ds(ca, 384)]
            x = pltpu.roll(x, 384 - cs, 1)[:, :N].reshape(33, 8, N)
            x = pltpu.roll(x, 8 - rs, 1)
            patch[comp] = jnp.where(sub < 8 - rs, x[:32], x[1:]).reshape(N, N)

        def stage_a(m):
            for i in range(0, H, 16):
                er, ei = [], []
                for t in (i, H + i):
                    qr, qi = probe[0, m, t : t + 16], probe[1, m, t : t + 16]
                    xr, xi = patch[0, t : t + 16], patch[1, t : t + 16]
                    er.append(qr * xr - qi * xi)
                    ei.append(qr * xi + qi * xr)
                for p in (0, 1):
                    for at, e in ((i, er), (H + i, ei)):
                        hi, lo = split(e[0] + e[1] if p == 0 else e[0] - e[1])
                        xa[m % 2, p, at : at + 16] = hi
                        xa[m % 2, p, N + at : N + at + 16] = lo

        def stage_b(m):
            return [dot(left[p], twice(xa[m % 2, p], 0)) for p in (0, 1)]

        def stage_c(m, L):
            for p in (0, 1):
                for i in range(0, H, 16):
                    re, im = L[p][i : i + 16], L[p][H + i : H + i + 16]
                    at = slice(p * H + i, p * H + i + 16)
                    for q in (0, 1):
                        for lane, e in ((0, re), (H, im)):
                            f = e[:, :H] + e[:, H:] if q == 0 else e[:, :H] - e[:, H:]
                            hi, lo = split(f)
                            xb[m % 2, q, at, lane : lane + H] = hi
                            xb[m % 2, q, at, N + lane : N + lane + H] = lo

        def stage_d(m):
            return [dot(twice(xb[m % 2, q], 1), rightT[q]) for q in (0, 1)]

        def stage_e(m, X):
            for q in (0, 1):
                for i in range(0, N, 16):
                    x = X[q][i : i + 16]
                    psi[m, q, i : i + 16] = x
                    e = x[:, :H] * x[:, :H] + x[:, H:] * x[:, H:]
                    before = -pats[s, q, i : i + 16] if m == 0 else res[q, i : i + 16]
                    res[q, i : i + 16] = before + e

        Ls, Xs = {}, {}
        stage_a(0)
        for t in range(6):
            if t < 4:
                Ls[t] = stage_b(t)
            if 0 <= t - 1 < 4:
                Xs[t - 1] = stage_d(t - 1)
            if t + 1 < 4:
                stage_a(t + 1)
            if t < 4:
                stage_c(t, Ls[t])
            if 0 <= t - 1 < 4:
                stage_e(t - 1, Xs[t - 1])

        def stage_f(m):
            for q in (0, 1):
                for i in range(0, N, 16):
                    w = res[q, i : i + 16]
                    x = psi[m, q, i : i + 16]
                    for lane in (0, H):
                        hi, lo = split(x[:, lane : lane + H] * w)
                        xc[m % 2, q, i : i + 16, lane : lane + H] = hi
                        xc[m % 2, q, i : i + 16, N + lane : N + lane + H] = lo

        def stage_g(m):
            return [dot(twice(xc[m % 2, q], 1), right[q]) for q in (0, 1)]

        def stage_i(m, T):
            for p in (0, 1):
                for i in range(0, H, 16):
                    t0, t1 = T[0][p * H + i : p * H + i + 16], T[1][p * H + i : p * H + i + 16]
                    for half, x in ((0, t0 + t1), (H, t0 - t1)):
                        for at, lane in ((i, 0), (H + i, H)):
                            hi, lo = split(x[:, lane : lane + H])
                            xd[m % 2, p, at : at + 16, half : half + H] = hi
                            xd[m % 2, p, N + at : N + at + 16, half : half + H] = lo

        def stage_j(m):
            return [dot(leftT[p], twice(xd[m % 2, p], 0)) for p in (0, 1)]

        def stage_k(m, L):
            for i in range(0, H, 8):
                for h, sign in ((0, 1), (H, -1)):
                    at = slice(h + i, h + i + 8)
                    if sign == 1:
                        br = L[0][i : i + 8] + L[1][i : i + 8]
                        bi = L[0][H + i : H + i + 8] + L[1][H + i : H + i + 8]
                    else:
                        br = L[0][i : i + 8] - L[1][i : i + 8]
                        bi = L[0][H + i : H + i + 8] - L[1][H + i : H + i + 8]
                    qr, qi = probe[0, m, at], probe[1, m, at]
                    xr, xi = patch[0, at], patch[1, at]
                    gr, gi = qr * br + qi * bi, qr * bi - qi * br
                    if m:
                        gr, gi = acc[0, at] + gr, acc[1, at] + gi
                    acc[0, at] = gr
                    acc[1, at] = gi
                    pgrad[0, m, at] += xr * br + xi * bi
                    pgrad[1, m, at] += xr * bi - xi * br

        Ts, Ls = {}, {}
        stage_f(0)
        loss_ref[...] += jnp.sum((res[0] * res[0] + res[1] * res[1]).reshape(32, 8, 128), axis=0)
        for t in range(6):
            if t < 4:
                Ts[t] = stage_g(t)
            if 0 <= t - 1 < 4:
                Ls[t - 1] = stage_j(t - 1)
            if t + 1 < 4:
                stage_f(t + 1)
            if t < 4:
                stage_i(t, Ts[t])
            if 0 <= t - 1 < 4:
                stage_k(t - 1, Ls[t - 1])

        for comp in (0, 1):
            x = pltpu.roll(acc[comp].reshape(32, 8, N), rs, 1)
            none = jnp.zeros((1, 8, N), jnp.float32)
            x = jnp.where(sub < rs, jnp.concatenate([none, x], axis=0), jnp.concatenate([x, none], axis=0))
            x = jnp.concatenate([x.reshape(264, N), jnp.zeros((264, H), jnp.float32)], axis=1)
            gext[comp, pl.ds(ra, 264), pl.ds(ca, 384)] += pltpu.roll(x, cs, 1)
        return 0

    lax.fori_loop(0, count, slot, 0)
    scans = lax.fori_loop(0, counts.shape[0], lambda i, t: t + counts[i], 0)
    loss_ref[...] = loss_ref[...] * (0.5 / (scans.astype(jnp.float32) * (N * N)))

    @pl.when(col == 15)
    def _():
        gext[:, :, 2 * N : 3 * N] = jnp.zeros((2, 776, N), jnp.float32)

    @pl.when(row == 7)
    def _():
        gext[:, 2 * N : 3 * N, :] = jnp.zeros((2, N, 896), jnp.float32)


def compute(counts, offsets, ext, probe, pats, *consts):
    V = pl.BlockSpec(memory_space=pltpu.VMEM)
    S = pl.BlockSpec(memory_space=pltpu.SMEM)
    return pl.pallas_call(
        compute_kernel,
        out_shape=(
            pltpu.VMEM((2, 776, 896), jnp.float32),
            pltpu.VMEM((2, 4, N, N), jnp.float32),
            jax.ShapeDtypeStruct((8, 128), jnp.float32),
        ),
        in_specs=[S, S] + [V] * 7,
        out_specs=(V, V, V),
        scratch_shapes=[
            pltpu.VMEM((2, N, N), jnp.float32),
            pltpu.VMEM((4, 2, N, N), jnp.float32),
            pltpu.VMEM((2, N, H), jnp.float32),
            pltpu.VMEM((2, N, N), jnp.float32),
            pltpu.VMEM((2, 2, 2 * N, N), jnp.bfloat16),
            pltpu.VMEM((2, 2, N, 2 * N), jnp.bfloat16),
            pltpu.VMEM((2, 2, N, 2 * N), jnp.bfloat16),
            pltpu.VMEM((2, 2, 2 * N, N), jnp.bfloat16),
        ],
        compiler_params=pltpu.CompilerParams(vmem_limit_bytes=16 << 20),
        name="compute",
    )(counts, offsets, ext, probe, pats, *consts)


MESH = pl.DeviceIdType.MESH
F32 = jnp.float32


def place():
    row = lax.axis_index("row")
    col = lax.axis_index("col")
    return col // 4, row // 2, col % 4, row % 2


def device_at(x, y, z, k):
    return (lax.rem(y + 8, 4) * 2 + k, lax.rem(x + 8, 4) * 4 + lax.rem(z + 8, 4))


def neighbours():
    row = lax.axis_index("row")
    col = lax.axis_index("col")
    left = (row, lax.rem(col + 15, 16))
    right = (row, lax.rem(col + 1, 16))
    above = (lax.rem(row + 7, 8), col)
    below = (lax.rem(row + 1, 8), col)
    return left, right, above, below


def groups():
    x, y, z, k = place()
    return {
        "k": [device_at(x, y, z, 1 - k)],
        "x": [device_at(x + d, y, z, k) for d in (1, 2, 3)],
        "y": [device_at(x, y + d, z, k) for d in (1, 2, 3)],
        "z": [device_at(x, y, z + d, k) for d in (1, 2, 3)],
    }


def greet(peers):
    barrier = pltpu.get_barrier_semaphore()
    for peer in peers:
        pl.semaphore_signal(barrier, inc=1, device_id=peer, device_id_type=MESH)
    pl.semaphore_wait(barrier, len(peers))


def remote(src, dst, send, recv, i, peer):
    copy = pltpu.make_async_remote_copy(
        src_ref=src, dst_ref=dst, send_sem=send.at[i], recv_sem=recv.at[i], device_id=peer, device_id_type=MESH
    )
    copy.start()
    return copy


class Small:
    def __init__(self, op, value, slots, send, recv, base):
        self.op, self.value, self.slots, self.send, self.recv, self.base = op, value, slots, send, recv, base
        self.step, self.at = 0, 0
        self.done = []

    def start(self):
        axis = "kxyz"[self.step]
        mine = dict(zip("xyzk", place()))[axis]
        self.slots[self.step, mine] = self.value[self.step]
        self.copies = []
        for peer in groups()[axis]:
            self.copies.append(
                remote(
                    self.value.at[self.step], self.slots.at[self.step, mine], self.send, self.recv,
                    self.base + self.at, peer,
                )
            )
            self.at += 1

    def finish(self):
        for copy in self.copies:
            copy.wait_recv()
        self.done += self.copies
        total = self.slots[self.step, 0]
        for i in range(1, len(self.copies) + 1):
            total = self.op(total, self.slots[self.step, i])
        self.step += 1
        self.value[self.step] = total


def halo_kernel(obj, probe, patterns, left_t, left_tt, right_t, right_tt, perm,
                ext, probe_v, pat_v, left_v, left_tv, right_v, right_tv, peak,
                raw, sort, swap, relay, local, send, recv):
    n = 256
    west, east, above, below = neighbours()
    x, y, z, k = place()
    up = device_at(x, y, z + 1, k)
    down = device_at(x, y, z - 1, k)
    end = device_at(x - jnp.where(z == 2, 1, 0), y, z + 1, k)
    origin = device_at(x + jnp.where(z == 3, 1, 0), y, z - 1, k)
    pairs = [
        (probe, probe_v), (patterns.at[0], raw), (perm, sort), (left_t, left_v), (left_tt, left_tv),
        (right_t, right_v), (right_tt, right_tv), (obj, ext.at[:, 0 : 2 * n, 0 : 2 * n]),
    ]
    loads = [pltpu.make_async_copy(src, dst, local.at[i]) for i, (src, dst) in enumerate(pairs)]
    greet([west, east, above, below, up, down, end, origin])
    top = remote(obj.at[:, 0:n, 0:n], ext.at[:, 0:n, 2 * n : 3 * n], send, recv, 0, west)
    side = remote(obj.at[:, 0:n, :], ext.at[:, 2 * n : 3 * n, 0 : 2 * n], send, recv, 2, above)
    first = [
        remote(obj.at[:, 384 + 64 * i : 448 + 64 * i, 0:n], relay.at[0, i], send, recv, 4 + i, up) for i in (0, 1)
    ]
    middle = remote(obj.at[:, n:384, 0:n], ext.at[:, n:384, 2 * n : 3 * n], send, recv, 1, west)
    for load in loads:
        load.start()
    for load in loads:
        load.wait()

    def largest(i, best):
        at = pl.ds(pl.multiple_of(i * 16, 16), 16)
        re = ext[0, at, 0 : 2 * n]
        im = ext[1, at, 0 : 2 * n]
        return jnp.maximum(best, re * re + im * im)

    best = lax.fori_loop(0, 32, largest, jnp.zeros((16, 512), F32))
    peak[...] = jnp.full((8, 128), jnp.max(best), F32)

    def order(s, _):
        hi, lo = split(raw[s])
        both = dot(hi, sort[...]) + dot(lo, sort[...])
        for q in (0, 1):
            swap[q] = both[:, q * H : (q + 1) * H]
        for q in (0, 1):
            for p in (0, 1):
                pat_v[s, q, p * H : (p + 1) * H, :] = swap[q, pl.ds(p, H, stride=2), :]
        return 0

    lax.fori_loop(0, 4, order, 0)
    second = []
    for i in (0, 1):
        first[i].wait_recv()
        second.append(remote(relay.at[0, i], relay.at[1, i], send, recv, 6 + i, up))
    top.wait_recv()
    corner = remote(ext.at[:, 0:n, 2 * n : 3 * n], ext.at[:, 2 * n : 3 * n, 2 * n : 3 * n], send, recv, 3, above)
    third = []
    for i in (0, 1):
        second[i].wait_recv()
        m = pl.ds(384 + 64 * i, 64)
        third.append(remote(relay.at[1, i], ext.at[:, m, 2 * n : 3 * n], send, recv, 8 + i, end))
    for copy in (side, middle, corner, *third):
        copy.wait_recv()
    for copy in (top, side, middle, corner, *first, *second, *third):
        copy.wait_send()

    @pl.when(lax.axis_index("col") == 15)
    def _():
        ext[:, :, 2 * n : 3 * n] = jnp.zeros((2, 776, n), F32)

    @pl.when(lax.axis_index("row") == 7)
    def _():
        ext[:, 2 * n : 3 * n, :] = jnp.zeros((2, n, 896), F32)


def halo(obj, probe, patterns):
    V = pl.BlockSpec(memory_space=pltpu.VMEM)
    A = pl.BlockSpec(memory_space=pltpu.HBM)
    consts = [jnp.asarray(t) for t in tables()]
    ins = [pltpu.with_memory_space_constraint(t, pltpu.HBM) for t in (obj, probe, patterns, *consts)]
    shapes = [(2, 776, 896), (2, 4, N, N), (4, 2, N, H)]
    outs = [pltpu.VMEM(s, F32) for s in shapes] + [pltpu.VMEM(t.shape, t.dtype) for t in consts[:4]]
    return pl.pallas_call(
        halo_kernel,
        out_shape=tuple(outs) + (jax.ShapeDtypeStruct((8, 128), F32),),
        in_specs=[A] * 8,
        out_specs=(V,) * 8,
        scratch_shapes=[
            pltpu.VMEM((4, N, N), F32),
            pltpu.VMEM((N, N), jnp.bfloat16),
            pltpu.VMEM((2, N, H), F32),
            pltpu.VMEM((2, 2, 2, 64, N), F32),
            pltpu.SemaphoreType.DMA((8,)),
            pltpu.SemaphoreType.DMA((10,)),
            pltpu.SemaphoreType.DMA((10,)),
        ],
        compiler_params=pltpu.CompilerParams(collective_id=0, has_side_effects=True, vmem_limit_bytes=16 << 20),
        name="halo",
    )(*ins)


PARTS = ((0, 384, "xyz"), (384, 256, "yzx"), (640, 384, "zxy"))


def exchange_kernel(gext, pg, obj, probe, peak, loss, new_obj, new_probe, loss_mean,
                    strip, corner, over, side, relay, r0, r1, r2, rz, value, slots, send, recv):
    n = 256
    left, right, above, below = neighbours()
    group = groups()
    x, y, z, k = place()
    index = {"x": x, "y": y, "z": z, "k": k}
    up, down = device_at(x, y, z + 1, k), device_at(x, y, z - 1, k)
    end = device_at(x + jnp.where(z == 1, 1, 0), y, z - 1, k)
    origin = device_at(x - jnp.where(z == 0, 1, 0), y, z + 1, k)
    counter = [0]

    def push(src, dst, peer):
        counter[0] += 1
        return remote(src, dst, send, recv, counter[0] - 1, peer)

    def rows(start, size):
        return pl.ds(pl.multiple_of(start, 8), size)

    def op(a, b):
        first = lax.broadcasted_iota(jnp.int32, (16, 128), 0) < 8
        return jnp.where(first, a + b, jnp.maximum(a, b))

    everyone = [group[a][i] for a in "kxyz" for i in range(len(group[a]))] + [left, right, above, below, up, down, end, origin]
    greet(everyone)
    sent = []
    over_sent, side_sent, corner_sent, rounds = [], [], [], ([], [], [])

    def push_corner(i):
        m = pl.ds(2 * n + 128 * i, 128)
        corner_sent.append(push(gext.at[:, m, 2 * n : 3 * n], corner.at[:, 128 * i : 128 * i + 128], below))

    def push_over(i):
        m = pl.ds(2 * n + 64 * i, 64)
        over_sent.append(push(gext.at[:, m, 0 : 2 * n], over.at[:, 64 * i : 64 * i + 64], below))

    def push_side(i):
        m = pl.ds(n + 64 * i, 64) if i < 2 else pl.ds(64 * i - 128, 64)
        source = gext.at[:, m, 2 * n : 3 * n] if i < 2 else strip.at[:, m]
        side_sent.append(push(source, side.at[:, m], right))

    def push_round(step, i):
        m = pl.ds(384 + 64 * i, 64)
        source = gext.at[:, m, 2 * n : 3 * n] if step == 0 else relay.at[step - 1, i]
        target = side.at[:, m] if step == 2 else relay.at[step, i]
        if step:
            rounds[step - 1][i].wait_recv()
        rounds[step].append(push(source, target, end if step == 2 else down))

    def fold_corner(i):
        corner_sent[i].wait_recv()
        m = pl.ds(128 * i, 128)
        strip[:, m] = gext[:, m, 2 * n : 3 * n] + corner[:, m]

    swap = []
    for first, size, _ in PARTS:
        swap.append(push(pg.at[rows((1 - k) * 1024 + first, size)], r0.at[first : first + size], group["k"][0]))
    push_corner(0)
    push_side(0)
    push_round(0, 0)
    value[0, 0:8] = loss[...]
    value[0, 8:16] = peak[...]
    small = Small(op, value, slots, send, recv, 84)
    small.start()

    steps = []
    for p, (first, size, axes) in enumerate(PARTS):
        swap[p].wait_recv()
        r0[first : first + size] += pg[rows(k * 1024 + first, size)]
        q = size // 4
        a = axes[0]
        copies = []
        for d, peer in enumerate(group[a]):
            other = lax.rem(index[a] + d + 1, 4)
            copies.append(push(r0.at[rows(first + other * q, q)], r1.at[d, first // 4 : first // 4 + q], peer))
        steps.append(copies)
    small.finish()
    small.start()
    push_corner(1)
    push_side(1)
    push_round(0, 1)
    second = []
    for p, (first, size, axes) in enumerate(PARTS):
        q, e = size // 4, size // 16
        a, b, c = axes
        f1, f2 = first // 4, first // 16
        for copy in steps[p]:
            copy.wait_recv()
        sent += steps[p]
        mine = rows(first + index[a] * q, q)
        r0[mine] += r1[0, f1 : f1 + q] + r1[1, f1 : f1 + q] + r1[2, f1 : f1 + q]
        copies = []
        for d, peer in enumerate(group[b]):
            other = lax.rem(index[b] + d + 1, 4)
            copies.append(push(r0.at[rows(first + index[a] * q + other * e, e)], r2.at[d, f2 : f2 + e], peer))
        second.append(copies)
    small.finish()
    small.start()
    push_over(0)
    fold_corner(0)
    push_side(2)
    push_round(1, 0)
    push_round(1, 1)
    third = []
    for p, (first, size, axes) in enumerate(PARTS):
        q, e = size // 4, size // 16
        a, b, c = axes
        f2 = first // 16
        for copy in second[p]:
            copy.wait_recv()
        sent += second[p]
        mine = rows(first + index[a] * q + index[b] * e, e)
        total = r0[mine] + r2[0, f2 : f2 + e] + r2[1, f2 : f2 + e] + r2[2, f2 : f2 + e]
        r0[mine] = total
        rz[index[c], f2 : f2 + e] = total
        third.append([push(r0.at[mine], rz.at[index[c], f2 : f2 + e], peer) for peer in group[c]])
    small.finish()
    small.start()
    push_over(1)
    fold_corner(1)
    push_side(3)
    small.finish()
    loss_mean[0, 0] = jnp.sum(value[4, 0:8])
    scale = 1.0 / value[4, 8:9, 0:1]

    back = []
    for p, (first, size, axes) in enumerate(PARTS):
        q, e = size // 4, size // 16
        a, b, c = axes
        f2 = first // 16
        for copy in third[p]:
            copy.wait_recv()
        sent += third[p]
        mine = rows(k * 1024 + first + index[a] * q + index[b] * e, e)
        total = ((rz[0, f2 : f2 + e] + rz[1, f2 : f2 + e]) + rz[2, f2 : f2 + e]) + rz[3, f2 : f2 + e]
        new_probe[mine] = probe[mine] - total * scale
        back.append([push(new_probe.at[mine], new_probe.at[mine], peer) for peer in group[b]])
    push_over(2)
    push_side(4)
    push_round(2, 0)
    push_round(2, 1)
    last = []
    for p, (first, size, axes) in enumerate(PARTS):
        q = size // 4
        a, b, c = axes
        for copy in back[p]:
            copy.wait_recv()
        sent += back[p]
        mine = rows(k * 1024 + first + index[a] * q, q)
        last.append([push(new_probe.at[mine], new_probe.at[mine], peer) for peer in group[a]])
    push_over(3)
    push_side(5)
    probe_peak = jnp.max(sum(probe[m * n : (m + 1) * n] * probe[m * n : (m + 1) * n] for m in range(8)))
    inverse = 1.0 / probe_peak
    new_obj[:, n : 2 * n, n : 2 * n] = obj[:, n : 2 * n, n : 2 * n] - gext[:, n : 2 * n, n : 2 * n] * inverse
    final = []
    for p, (first, size, axes) in enumerate(PARTS):
        for copy in last[p]:
            copy.wait_recv()
        sent += last[p]
        mine = rows(k * 1024 + first, size)
        final.append(push(new_probe.at[mine], new_probe.at[mine], group["k"][0]))
    for copy in over_sent:
        copy.wait_recv()
    new_obj[:, 0:n, n : 2 * n] = obj[:, 0:n, n : 2 * n] - (gext[:, 0:n, n : 2 * n] + over[:, :, n : 2 * n]) * inverse
    for copy in side_sent + rounds[2]:
        copy.wait_recv()
    sent += over_sent + side_sent + rounds[0] + rounds[1] + rounds[2] + corner_sent + swap + final + small.done
    new_obj[:, 0:n, 0:n] = obj[:, 0:n, 0:n] - (gext[:, 0:n, 0:n] + over[:, :, 0:n] + side[:, 0:n]) * inverse
    new_obj[:, n : 2 * n, 0:n] = obj[:, n : 2 * n, 0:n] - (gext[:, n : 2 * n, 0:n] + side[:, n : 2 * n]) * inverse
    for copy in final:
        copy.wait_recv()
    for copy in sent:
        copy.wait_send()


def exchange(gext, pg, obj, probe, peak, loss):
    V = pl.BlockSpec(memory_space=pltpu.VMEM)
    S = pl.BlockSpec(memory_space=pltpu.SMEM)
    new_obj, new_probe, loss_mean = pl.pallas_call(
        exchange_kernel,
        out_shape=(
            jax.ShapeDtypeStruct((2, 512, 512), F32),
            jax.ShapeDtypeStruct((2048, 256), F32),
            jax.ShapeDtypeStruct((1, 1), F32),
        ),
        in_specs=[V] * 6,
        out_specs=(V, V, S),
        scratch_shapes=[
            pltpu.VMEM((2, 256, 256), F32),
            pltpu.VMEM((2, 256, 256), F32),
            pltpu.VMEM((2, 256, 512), F32),
            pltpu.VMEM((2, 512, 256), F32),
            pltpu.VMEM((2, 2, 2, 64, 256), F32),
            pltpu.VMEM((1024, 256), F32),
            pltpu.VMEM((3, 256, 256), F32),
            pltpu.VMEM((3, 64, 256), F32),
            pltpu.VMEM((4, 64, 256), F32),
            pltpu.VMEM((5, 16, 128), F32),
            pltpu.VMEM((4, 4, 16, 128), F32),
            pltpu.SemaphoreType.DMA((96,)),
            pltpu.SemaphoreType.DMA((96,)),
        ],
        compiler_params=pltpu.CompilerParams(collective_id=1, has_side_effects=True, vmem_limit_bytes=30 << 20),
        name="exchange",
    )(gext, pg.reshape(2048, 256), obj, probe.reshape(2048, 256), peak, loss)
    return new_obj, new_probe.reshape(probe.shape), loss_mean.reshape(())


def body(object_slab, probe_field, patterns, offsets, counts):
    ext, probe, pats, left, left_t, right, right_t, peak = halo(object_slab, probe_field, patterns)
    gext, pg, loss = compute(counts, jnp.swapaxes(offsets, 1, 2), ext, probe, pats, left, left_t, right, right_t)
    return exchange(gext, pg, ext, probe, peak, loss)


def solution(mesh):
    placed = (
        P(None, "row", "col"),
        P(),
        P(("row", "col"), None, None, None),
        P(("row", "col"), None, None),
        P(),
    )
    return jax.shard_map(
        body,
        mesh=mesh,
        in_specs=placed,
        out_specs=(P(None, "row", "col"), P(), P()),
        check_vma=False,
    )
```

```python
import math

import jax
import jax.numpy as jnp
import ml_dtypes
import numpy as np
from jax import lax
from jax.experimental import pallas as pl
from jax.experimental.pallas import tpu as pltpu
from jax.sharding import PartitionSpec as P

N = 256
H = 128


def split(x):
    hi = x.astype(jnp.bfloat16)
    lo = (x - hi.astype(jnp.float32)).astype(jnp.bfloat16)
    return hi, lo

def tables():
    k = np.arange(H)[:, None]
    n = np.arange(H)[None, :]
    out = []
    for q in (0, 1):
        ph = -2.0 * math.pi * ((n * (2 * k + q)) % N) / N
        c, s = np.cos(ph) / 16.0, np.sin(ph) / 16.0
        out.append(np.block([[c, -s], [s, c]]))
    t = np.stack(out).astype(np.float32)
    def hl(a):
        hi = a.astype(ml_dtypes.bfloat16)
        lo = (a - hi.astype(np.float32)).astype(ml_dtypes.bfloat16)
        return hi, lo
    hi, lo = hl(t)
    left = np.concatenate([hi, hi, lo], axis=2)
    hiT, loT = hi.transpose(0, 2, 1), lo.transpose(0, 2, 1)
    leftT = np.concatenate([hiT, hiT, loT], axis=2)
    right = np.concatenate([hi, hi, lo], axis=1)
    rightT = np.concatenate([hiT, hiT, loT], axis=1)
    perm = np.zeros((N, N), np.float32)
    for i in range(H):
        perm[2 * i, i] = 1; perm[2 * i + 1, H + i] = 1
    return left, leftT, right, rightT, perm.astype(ml_dtypes.bfloat16)

def dot(a, b):
    return jnp.dot(a, b, preferred_element_type=jnp.float32)

def lmul(t, x):
    hi, lo = split(x)
    return dot(t, jnp.concatenate([hi, lo, hi], axis=0))

def rmul(x, t):
    hi, lo = split(x)
    return dot(jnp.concatenate([hi, lo, hi], axis=1), t)

def twice(a, axis):
    return jnp.concatenate([a, lax.slice_in_dim(a, 0, N, axis=axis)], axis=axis)


def compute_kernel(counts, offsets, ext, probe, pats, left, leftT, right, rightT, gext_in, pgrad_in,
                   gext, pgrad, loss_ref, patch, psi, res, acc, xa, xb, xc, xd):
    row = lax.axis_index("row")
    col = lax.axis_index("col")
    count = counts[row * 16 + col]
    loss_ref[...] = jnp.zeros_like(loss_ref)

    def slot(s, _):
        r = offsets[0, 0, s]
        c = offsets[0, 1, s]
        ca = pl.multiple_of(c // 128 * 128, 128)
        cs = c - ca
        ra = pl.multiple_of(r // 8 * 8, 8)
        rs = r - ra
        sub = lax.broadcasted_iota(jnp.int32, (1, 8, H), 1)
        lane = lax.broadcasted_iota(jnp.int32, (1, H), 1)
        for comp in (0, 1):
            x = ext[comp, pl.ds(ra, 264), pl.ds(ca, 384)]
            x = [pltpu.roll(x[:, i * H : i * H + H], H - cs, 1) for i in range(3)]
            for i in range(2):
                y = jnp.where(lane < H - cs, x[i], x[i + 1]).reshape(33, 8, H)
                y = pltpu.roll(y, 8 - rs, 1)
                patch[comp, :, i * H : i * H + H] = jnp.where(sub < 8 - rs, y[:32], y[1:]).reshape(N, H)

        def stage_a(m):
            for i in range(0, H, 16):
                er, ei = [], []
                for t in (i, H + i):
                    qr, qi = probe[0, m, t : t + 16], probe[1, m, t : t + 16]
                    xr, xi = patch[0, t : t + 16], patch[1, t : t + 16]
                    er.append(qr * xr - qi * xi)
                    ei.append(qr * xi + qi * xr)
                for p in (0, 1):
                    for at, e in ((i, er), (H + i, ei)):
                        hi, lo = split(e[0] + e[1] if p == 0 else e[0] - e[1])
                        xa[m % 2, p, at : at + 16] = hi
                        xa[m % 2, p, N + at : N + at + 16] = lo

        def stage_b(m):
            return [dot(left[p], twice(xa[m % 2, p], 0)) for p in (0, 1)]

        def stage_c(m, L):
            for p in (0, 1):
                for i in range(0, H, 16):
                    re, im = L[p][i : i + 16], L[p][H + i : H + i + 16]
                    at = slice(p * H + i, p * H + i + 16)
                    for q in (0, 1):
                        for lane, e in ((0, re), (H, im)):
                            f = e[:, :H] + e[:, H:] if q == 0 else e[:, :H] - e[:, H:]
                            hi, lo = split(f)
                            xb[m % 2, q, at, lane : lane + H] = hi
                            xb[m % 2, q, at, N + lane : N + lane + H] = lo

        def stage_d(m):
            return [dot(twice(xb[m % 2, q], 1), rightT[q]) for q in (0, 1)]

        def stage_e(m, X):
            for q in (0, 1):
                for i in range(0, N, 16):
                    x = X[q][i : i + 16]
                    psi[m, q, i : i + 16] = x
                    e = x[:, :H] * x[:, :H] + x[:, H:] * x[:, H:]
                    before = -pats[s, q, i : i + 16] if m == 0 else res[q, i : i + 16]
                    res[q, i : i + 16] = before + e

        Ls, Xs = {}, {}
        stage_a(0)
        for t in range(6):
            if t < 4:
                Ls[t] = stage_b(t)
            if 0 <= t - 1 < 4:
                Xs[t - 1] = stage_d(t - 1)
            if t + 1 < 4:
                stage_a(t + 1)
            if t < 4:
                stage_c(t, Ls[t])
            if 0 <= t - 1 < 4:
                stage_e(t - 1, Xs[t - 1])

        def stage_f(m):
            for q in (0, 1):
                for i in range(0, N, 16):
                    w = res[q, i : i + 16]
                    x = psi[m, q, i : i + 16]
                    for lane in (0, H):
                        hi, lo = split(x[:, lane : lane + H] * w)
                        xc[m % 2, q, i : i + 16, lane : lane + H] = hi
                        xc[m % 2, q, i : i + 16, N + lane : N + lane + H] = lo

        def stage_g(m):
            return [dot(twice(xc[m % 2, q], 1), right[q]) for q in (0, 1)]

        def stage_i(m, T):
            for p in (0, 1):
                for i in range(0, H, 16):
                    t0, t1 = T[0][p * H + i : p * H + i + 16], T[1][p * H + i : p * H + i + 16]
                    for half, x in ((0, t0 + t1), (H, t0 - t1)):
                        for at, lane in ((i, 0), (H + i, H)):
                            hi, lo = split(x[:, lane : lane + H])
                            xd[m % 2, p, at : at + 16, half : half + H] = hi
                            xd[m % 2, p, N + at : N + at + 16, half : half + H] = lo

        def stage_j(m):
            return [dot(leftT[p], twice(xd[m % 2, p], 0)) for p in (0, 1)]

        def stage_k(m, L):
            for i in range(0, H, 8):
                for h, sign in ((0, 1), (H, -1)):
                    at = slice(h + i, h + i + 8)
                    if sign == 1:
                        br = L[0][i : i + 8] + L[1][i : i + 8]
                        bi = L[0][H + i : H + i + 8] + L[1][H + i : H + i + 8]
                    else:
                        br = L[0][i : i + 8] - L[1][i : i + 8]
                        bi = L[0][H + i : H + i + 8] - L[1][H + i : H + i + 8]
                    qr, qi = probe[0, m, at], probe[1, m, at]
                    xr, xi = patch[0, at], patch[1, at]
                    gr, gi = qr * br + qi * bi, qr * bi - qi * br
                    if m:
                        gr, gi = acc[0, at] + gr, acc[1, at] + gi
                    acc[0, at] = gr
                    acc[1, at] = gi
                    pgrad[0, m, at] += xr * br + xi * bi
                    pgrad[1, m, at] += xr * bi - xi * br

        Ts, Ls = {}, {}
        stage_f(0)
        loss_ref[...] += jnp.sum((res[0] * res[0] + res[1] * res[1]).reshape(32, 8, 128), axis=0)
        for t in range(6):
            if t < 4:
                Ts[t] = stage_g(t)
            if 0 <= t - 1 < 4:
                Ls[t - 1] = stage_j(t - 1)
            if t + 1 < 4:
                stage_f(t + 1)
            if t < 4:
                stage_i(t, Ts[t])
            if 0 <= t - 1 < 4:
                stage_k(t - 1, Ls[t - 1])

        for comp in (0, 1):
            none = jnp.zeros((1, 8, H), jnp.float32)
            blank = jnp.zeros((264, H), jnp.float32)
            x = []
            for i in range(2):
                y = pltpu.roll(acc[comp, :, i * H : i * H + H].reshape(32, 8, H), rs, 1)
                y = jnp.where(sub < rs, jnp.concatenate([none, y], axis=0), jnp.concatenate([y, none], axis=0))
                x.append(pltpu.roll(y.reshape(264, H), cs, 1))
            x = [blank, x[0], x[1], blank]
            for i in range(3):
                at = pl.ds(pl.multiple_of(ca + i * H, H), H)
                gext[comp, pl.ds(ra, 264), at] += jnp.where(lane < cs, x[i], x[i + 1])
        return 0

    lax.fori_loop(0, count, slot, 0)
    scans = lax.fori_loop(0, counts.shape[0], lambda i, t: t + counts[i], 0)
    loss_ref[...] = loss_ref[...] * (0.5 / (scans.astype(jnp.float32) * (N * N)))

    @pl.when(col == 15)
    def _():
        gext[:, :, 2 * N : 3 * N] = jnp.zeros((2, 776, N), jnp.float32)

    @pl.when(row == 7)
    def _():
        gext[:, 2 * N : 3 * N, :] = jnp.zeros((2, N, 896), jnp.float32)


def compute(counts, offsets, ext, probe, pats, *consts):
    V = pl.BlockSpec(memory_space=pltpu.VMEM)
    S = pl.BlockSpec(memory_space=pltpu.SMEM)
    return pl.pallas_call(
        compute_kernel,
        out_shape=(
            pltpu.VMEM((2, 776, 896), jnp.float32),
            pltpu.VMEM((2, 4, N, N), jnp.float32),
            jax.ShapeDtypeStruct((8, 128), jnp.float32),
        ),
        in_specs=[S, S] + [V] * 9,
        out_specs=(V, V, V),
        input_output_aliases={9: 0, 10: 1},
        scratch_shapes=[
            pltpu.VMEM((2, N, N), jnp.float32),
            pltpu.VMEM((4, 2, N, N), jnp.float32),
            pltpu.VMEM((2, N, H), jnp.float32),
            pltpu.VMEM((2, N, N), jnp.float32),
            pltpu.VMEM((2, 2, 2 * N, N), jnp.bfloat16),
            pltpu.VMEM((2, 2, N, 2 * N), jnp.bfloat16),
            pltpu.VMEM((2, 2, N, 2 * N), jnp.bfloat16),
            pltpu.VMEM((2, 2, 2 * N, N), jnp.bfloat16),
        ],
        compiler_params=pltpu.CompilerParams(vmem_limit_bytes=16 << 20),
        name="compute",
    )(counts, offsets, ext, probe, pats, *consts)


MESH = pl.DeviceIdType.MESH
F32 = jnp.float32


def place():
    row = lax.axis_index("row")
    col = lax.axis_index("col")
    return col // 4, row // 2, col % 4, row % 2


def device_at(x, y, z, k):
    return (lax.rem(y + 8, 4) * 2 + k, lax.rem(x + 8, 4) * 4 + lax.rem(z + 8, 4))


def neighbours():
    row = lax.axis_index("row")
    col = lax.axis_index("col")
    left = (row, lax.rem(col + 15, 16))
    right = (row, lax.rem(col + 1, 16))
    above = (lax.rem(row + 7, 8), col)
    below = (lax.rem(row + 1, 8), col)
    return left, right, above, below


def groups():
    x, y, z, k = place()
    return {
        "k": [device_at(x, y, z, 1 - k)],
        "x": [device_at(x + d, y, z, k) for d in (1, 2, 3)],
        "y": [device_at(x, y + d, z, k) for d in (1, 2, 3)],
        "z": [device_at(x, y, z + d, k) for d in (1, 2, 3)],
    }


def greet(peers):
    barrier = pltpu.get_barrier_semaphore()
    for peer in peers:
        pl.semaphore_signal(barrier, inc=1, device_id=peer, device_id_type=MESH)
    pl.semaphore_wait(barrier, len(peers))


def remote(src, dst, send, recv, i, peer):
    copy = pltpu.make_async_remote_copy(
        src_ref=src, dst_ref=dst, send_sem=send.at[i], recv_sem=recv.at[i], device_id=peer, device_id_type=MESH
    )
    copy.start()
    return copy


class Small:
    def __init__(self, op, value, slots, send, recv, base):
        self.op, self.value, self.slots, self.send, self.recv, self.base = op, value, slots, send, recv, base
        self.step, self.at = 0, 0
        self.done = []

    def start(self):
        axis = "kxyz"[self.step]
        mine = dict(zip("xyzk", place()))[axis]
        self.slots[self.step, mine] = self.value[self.step]
        self.copies = []
        for peer in groups()[axis]:
            self.copies.append(
                remote(
                    self.value.at[self.step], self.slots.at[self.step, mine], self.send, self.recv,
                    self.base + self.at, peer,
                )
            )
            self.at += 1

    def finish(self):
        for copy in self.copies:
            copy.wait_recv()
        self.done += self.copies
        total = self.slots[self.step, 0]
        for i in range(1, len(self.copies) + 1):
            total = self.op(total, self.slots[self.step, i])
        self.step += 1
        self.value[self.step] = total


def halo_kernel(obj, probe, patterns, left_t, left_tt, right_t, right_tt, perm,
                ext, probe_v, pat_v, left_v, left_tv, right_v, right_tv, gext, pgrad, peak,
                raw, sort, swap, relay, local, send, recv):
    n = 256
    west, east, above, below = neighbours()
    x, y, z, k = place()
    up = device_at(x, y, z + 1, k)
    down = device_at(x, y, z - 1, k)
    end = device_at(x - jnp.where(z == 2, 1, 0), y, z + 1, k)
    origin = device_at(x + jnp.where(z == 3, 1, 0), y, z - 1, k)
    pairs = [
        (probe, probe_v), (patterns.at[0], raw), (perm, sort), (left_t, left_v), (left_tt, left_tv),
        (right_t, right_v), (right_tt, right_tv), (obj, ext.at[:, 0 : 2 * n, 0 : 2 * n]),
    ]
    loads = [pltpu.make_async_copy(src, dst, local.at[i]) for i, (src, dst) in enumerate(pairs)]
    greet([west, east, above, below, up, down, end, origin])
    top = [
        remote(obj.at[:, m : m + H, 0:n], ext.at[:, m : m + H, 2 * n : 3 * n], send, recv, i, west)
        for i, m in ((0, 0), (3, H))
    ]
    side = remote(obj.at[:, 0:n, :], ext.at[:, 2 * n : 3 * n, 0 : 2 * n], send, recv, 2, above)
    first = [
        remote(obj.at[:, 384 + 64 * i : 448 + 64 * i, 0:n], relay.at[0, i], send, recv, 4 + i, up) for i in (0, 1)
    ]
    middle = remote(obj.at[:, n:384, 0:n], ext.at[:, n:384, 2 * n : 3 * n], send, recv, 1, west)
    for load in loads:
        load.start()
    gext[...] = jnp.zeros_like(gext)
    pgrad[...] = jnp.zeros_like(pgrad)
    for load in loads:
        load.wait()

    def largest(i, best):
        at = pl.ds(pl.multiple_of(i * 16, 16), 16)
        re = ext[0, at, 0 : 2 * n]
        im = ext[1, at, 0 : 2 * n]
        return jnp.maximum(best, re * re + im * im)

    best = lax.fori_loop(0, 32, largest, jnp.zeros((16, 512), F32))
    peak[...] = jnp.full((8, 128), jnp.max(best), F32)

    def order(s, _):
        hi, lo = split(raw[s])
        both = dot(hi, sort[...]) + dot(lo, sort[...])
        for q in (0, 1):
            swap[q] = both[:, q * H : (q + 1) * H]
        for q in (0, 1):
            for p in (0, 1):
                pat_v[s, q, p * H : (p + 1) * H, :] = swap[q, pl.ds(p, H, stride=2), :]
        return 0

    lax.fori_loop(0, 4, order, 0)
    second, corner = [], []
    for i in (0, 1):
        first[i].wait_recv()
        second.append(remote(relay.at[0, i], relay.at[1, i], send, recv, 6 + i, up))
        top[i].wait_recv()
        m = i * H
        corner.append(
            remote(
                ext.at[:, m : m + H, 2 * n : 3 * n], ext.at[:, 2 * n + m : 2 * n + m + H, 2 * n : 3 * n],
                send, recv, 10 + i, above,
            )
        )
    third = []
    for i in (0, 1):
        second[i].wait_recv()
        m = pl.ds(384 + 64 * i, 64)
        third.append(remote(relay.at[1, i], ext.at[:, m, 2 * n : 3 * n], send, recv, 8 + i, end))
    for copy in (side, middle, *corner, *third):
        copy.wait_recv()
    for copy in (*top, side, middle, *corner, *first, *second, *third):
        copy.wait_send()

    @pl.when(lax.axis_index("col") == 15)
    def _():
        ext[:, :, 2 * n : 3 * n] = jnp.zeros((2, 776, n), F32)

    @pl.when(lax.axis_index("row") == 7)
    def _():
        ext[:, 2 * n : 3 * n, :] = jnp.zeros((2, n, 896), F32)


def halo(obj, probe, patterns):
    V = pl.BlockSpec(memory_space=pltpu.VMEM)
    A = pl.BlockSpec(memory_space=pltpu.HBM)
    consts = [jnp.asarray(t) for t in tables()]
    ins = [pltpu.with_memory_space_constraint(t, pltpu.HBM) for t in (obj, probe, patterns, *consts)]
    shapes = [(2, 776, 896), (2, 4, N, N), (4, 2, N, H)]
    outs = [pltpu.VMEM(s, F32) for s in shapes] + [pltpu.VMEM(t.shape, t.dtype) for t in consts[:4]]
    outs += [pltpu.VMEM(s, F32) for s in shapes[:2]]
    return pl.pallas_call(
        halo_kernel,
        out_shape=tuple(outs) + (jax.ShapeDtypeStruct((8, 128), F32),),
        in_specs=[A] * 8,
        out_specs=(V,) * 10,
        scratch_shapes=[
            pltpu.VMEM((4, N, N), F32),
            pltpu.VMEM((N, N), jnp.bfloat16),
            pltpu.VMEM((2, N, H), F32),
            pltpu.VMEM((2, 2, 2, 64, N), F32),
            pltpu.SemaphoreType.DMA((8,)),
            pltpu.SemaphoreType.DMA((12,)),
            pltpu.SemaphoreType.DMA((12,)),
        ],
        compiler_params=pltpu.CompilerParams(collective_id=0, has_side_effects=True, vmem_limit_bytes=16 << 20),
        name="halo",
    )(*ins)


PARTS = ((0, 128, "xyz"), (128, 128, "yzx"), (256, 128, "zxy"), (384, 256, "xyz"), (640, 128, "yzx"), (768, 256, "zxy"))


def exchange_kernel(gext, pg, obj, probe, peak, loss, new_obj, new_probe, loss_mean,
                    strip, corner, over, side, relay, r0, r1, r2, rz, value, slots, send, recv):
    n = 256
    left, right, above, below = neighbours()
    group = groups()
    x, y, z, k = place()
    index = {"x": x, "y": y, "z": z, "k": k}
    up, down = device_at(x, y, z + 1, k), device_at(x, y, z - 1, k)
    end = device_at(x + jnp.where(z == 1, 1, 0), y, z - 1, k)
    origin = device_at(x - jnp.where(z == 0, 1, 0), y, z + 1, k)
    counter = [0]

    def push(src, dst, peer):
        counter[0] += 1
        return remote(src, dst, send, recv, counter[0] - 1, peer)

    def rows(start, size):
        return pl.ds(pl.multiple_of(start, 8), size)

    def op(a, b):
        first = lax.broadcasted_iota(jnp.int32, (16, 128), 0) < 8
        return jnp.where(first, a + b, jnp.maximum(a, b))

    everyone = [group[a][i] for a in "kxyz" for i in range(len(group[a]))] + [left, right, above, below, up, down, end, origin]
    greet(everyone)
    sent = []
    over_sent, side_sent, corner_sent, rounds = [], [], [], ([], [], [])

    def push_corner(i):
        m = pl.ds(2 * n + 128 * i, 128)
        corner_sent.append(push(gext.at[:, m, 2 * n : 3 * n], corner.at[:, 128 * i : 128 * i + 128], below))

    def push_over(i):
        m = pl.ds(2 * n + 64 * i, 64)
        over_sent.append(push(gext.at[:, m, 0 : 2 * n], over.at[:, 64 * i : 64 * i + 64], below))

    def push_side(i):
        m = pl.ds(n + 64 * i, 64) if i < 2 else pl.ds(64 * i - 128, 64)
        source = gext.at[:, m, 2 * n : 3 * n] if i < 2 else strip.at[:, m]
        side_sent.append(push(source, side.at[:, m], right))

    def push_round(step, i):
        m = pl.ds(384 + 64 * i, 64)
        source = gext.at[:, m, 2 * n : 3 * n] if step == 0 else relay.at[step - 1, i]
        target = side.at[:, m] if step == 2 else relay.at[step, i]
        if step:
            rounds[step - 1][i].wait_recv()
        rounds[step].append(push(source, target, end if step == 2 else down))

    def fold_corner(i):
        corner_sent[i].wait_recv()
        m = pl.ds(128 * i, 128)
        strip[:, m] = gext[:, m, 2 * n : 3 * n] + corner[:, m]

    swap = []
    for first, size, _ in PARTS:
        swap.append(push(pg.at[rows((1 - k) * 1024 + first, size)], r0.at[first : first + size], group["k"][0]))
    push_corner(0)
    push_side(0)
    push_round(0, 0)
    value[0, 0:8] = loss[...]
    value[0, 8:16] = peak[...]
    small = Small(op, value, slots, send, recv, 200)
    small.start()

    steps = []
    for p, (first, size, axes) in enumerate(PARTS):
        swap[p].wait_recv()
        r0[first : first + size] += pg[rows(k * 1024 + first, size)]
        q = size // 4
        a = axes[0]
        copies = []
        for d, peer in enumerate(group[a]):
            other = lax.rem(index[a] + d + 1, 4)
            copies.append(push(r0.at[rows(first + other * q, q)], r1.at[d, first // 4 : first // 4 + q], peer))
        steps.append(copies)
    small.finish()
    small.start()
    push_corner(1)
    push_side(1)
    push_round(0, 1)
    second = []
    for p, (first, size, axes) in enumerate(PARTS):
        q, e = size // 4, size // 16
        a, b, c = axes
        f1, f2 = first // 4, first // 16
        for copy in steps[p]:
            copy.wait_recv()
        sent += steps[p]
        mine = rows(first + index[a] * q, q)
        r0[mine] += r1[0, f1 : f1 + q] + r1[1, f1 : f1 + q] + r1[2, f1 : f1 + q]
        copies = []
        for d, peer in enumerate(group[b]):
            other = lax.rem(index[b] + d + 1, 4)
            copies.append(push(r0.at[rows(first + index[a] * q + other * e, e)], r2.at[d, f2 : f2 + e], peer))
        second.append(copies)
    small.finish()
    small.start()
    push_over(0)
    fold_corner(0)
    push_side(2)
    push_round(1, 0)
    push_round(1, 1)
    third = []
    for p, (first, size, axes) in enumerate(PARTS):
        q, e = size // 4, size // 16
        a, b, c = axes
        f2 = first // 16
        for copy in second[p]:
            copy.wait_recv()
        sent += second[p]
        mine = rows(first + index[a] * q + index[b] * e, e)
        total = r0[mine] + r2[0, f2 : f2 + e] + r2[1, f2 : f2 + e] + r2[2, f2 : f2 + e]
        r0[mine] = total
        rz[index[c], f2 : f2 + e] = total
        third.append([push(r0.at[mine], rz.at[index[c], f2 : f2 + e], peer) for peer in group[c]])
    small.finish()
    small.start()
    push_over(1)
    fold_corner(1)
    push_side(3)
    small.finish()
    loss_mean[0, 0] = jnp.sum(value[4, 0:8])
    scale = 1.0 / value[4, 8:9, 0:1]

    back = []
    for p, (first, size, axes) in enumerate(PARTS):
        q, e = size // 4, size // 16
        a, b, c = axes
        f2 = first // 16
        for copy in third[p]:
            copy.wait_recv()
        sent += third[p]
        mine = rows(k * 1024 + first + index[a] * q + index[b] * e, e)
        total = ((rz[0, f2 : f2 + e] + rz[1, f2 : f2 + e]) + rz[2, f2 : f2 + e]) + rz[3, f2 : f2 + e]
        new_probe[mine] = probe[mine] - total * scale
        back.append([push(new_probe.at[mine], new_probe.at[mine], peer) for peer in group[b]])
    push_over(2)
    push_side(4)
    push_round(2, 0)
    push_round(2, 1)
    last = []
    for p, (first, size, axes) in enumerate(PARTS):
        q, e = size // 4, size // 16
        a, b, c = axes
        copies = []
        for d in range(4):
            if d:
                back[p][d - 1].wait_recv()
            mine = rows(k * 1024 + first + index[a] * q + lax.rem(index[b] + 4 - d, 4) * e, e)
            copies.append([push(new_probe.at[mine], new_probe.at[mine], peer) for peer in group[a]])
        sent += back[p]
        last.append(copies)
    push_over(3)
    push_side(5)
    probe_peak = jnp.max(sum(probe[m * n : (m + 1) * n] * probe[m * n : (m + 1) * n] for m in range(8)))
    inverse = 1.0 / probe_peak
    new_obj[:, n : 2 * n, n : 2 * n] = obj[:, n : 2 * n, n : 2 * n] - gext[:, n : 2 * n, n : 2 * n] * inverse
    final = []
    for p, (first, size, axes) in enumerate(PARTS):
        q = size // 4
        a, b, c = axes
        for d in range(4):
            if d:
                for copies in last[p]:
                    copies[d - 1].wait_recv()
            mine = rows(k * 1024 + first + lax.rem(index[a] + 4 - d, 4) * q, q)
            final.append(push(new_probe.at[mine], new_probe.at[mine], group["k"][0]))
        for copies in last[p]:
            sent += copies
    for copy in over_sent:
        copy.wait_recv()
    new_obj[:, 0:n, n : 2 * n] = obj[:, 0:n, n : 2 * n] - (gext[:, 0:n, n : 2 * n] + over[:, :, n : 2 * n]) * inverse
    for copy in side_sent + rounds[2]:
        copy.wait_recv()
    sent += over_sent + side_sent + rounds[0] + rounds[1] + rounds[2] + corner_sent + swap + final + small.done
    new_obj[:, 0:n, 0:n] = obj[:, 0:n, 0:n] - (gext[:, 0:n, 0:n] + over[:, :, 0:n] + side[:, 0:n]) * inverse
    new_obj[:, n : 2 * n, 0:n] = obj[:, n : 2 * n, 0:n] - (gext[:, n : 2 * n, 0:n] + side[:, n : 2 * n]) * inverse
    for copy in final:
        copy.wait_recv()
    for copy in sent:
        copy.wait_send()


def exchange(gext, pg, obj, probe, peak, loss):
    V = pl.BlockSpec(memory_space=pltpu.VMEM)
    S = pl.BlockSpec(memory_space=pltpu.SMEM)
    new_obj, new_probe, loss_mean = pl.pallas_call(
        exchange_kernel,
        out_shape=(
            pltpu.VMEM((2, 512, 512), F32),
            pltpu.VMEM((2048, 256), F32),
            jax.ShapeDtypeStruct((1, 1), F32),
        ),
        in_specs=[V] * 6,
        out_specs=(V, V, S),
        scratch_shapes=[
            pltpu.VMEM((2, 256, 256), F32),
            pltpu.VMEM((2, 256, 256), F32),
            pltpu.VMEM((2, 256, 512), F32),
            pltpu.VMEM((2, 512, 256), F32),
            pltpu.VMEM((2, 2, 2, 64, 256), F32),
            pltpu.VMEM((1024, 256), F32),
            pltpu.VMEM((3, 256, 256), F32),
            pltpu.VMEM((3, 64, 256), F32),
            pltpu.VMEM((4, 64, 256), F32),
            pltpu.VMEM((5, 16, 128), F32),
            pltpu.VMEM((4, 4, 16, 128), F32),
            pltpu.SemaphoreType.DMA((212,)),
            pltpu.SemaphoreType.DMA((212,)),
        ],
        compiler_params=pltpu.CompilerParams(collective_id=1, has_side_effects=True, vmem_limit_bytes=30 << 20),
        name="exchange",
    )(gext, pg.reshape(2048, 256), obj, probe.reshape(2048, 256), peak, loss)
    return new_obj, new_probe, loss_mean


def finish_kernel(new_obj, new_probe, loss_mean, obj_out, probe_out, loss_out, sems):
    copies = []
    for i in range(4):
        m = pl.ds(128 * i, 128)
        copies.append(pltpu.make_async_copy(new_obj.at[:, m], obj_out.at[:, m], sems.at[i]))
        m = pl.ds(512 * i, 512)
        copies.append(pltpu.make_async_copy(new_probe.at[m], probe_out.at[m], sems.at[4 + i]))
    for copy in copies:
        copy.start()
    loss_out[0, 0] = loss_mean[0, 0]
    for copy in copies:
        copy.wait()


def finish(new_obj, new_probe, loss_mean):
    V = pl.BlockSpec(memory_space=pltpu.VMEM)
    A = pl.BlockSpec(memory_space=pltpu.HBM)
    S = pl.BlockSpec(memory_space=pltpu.SMEM)
    return pl.pallas_call(
        finish_kernel,
        out_shape=(
            pltpu.HBM(new_obj.shape, F32),
            pltpu.HBM(new_probe.shape, F32),
            jax.ShapeDtypeStruct((1, 1), F32),
        ),
        in_specs=[V, V, S],
        out_specs=(A, A, S),
        scratch_shapes=[pltpu.SemaphoreType.DMA((8,))],
        compiler_params=pltpu.CompilerParams(vmem_limit_bytes=6 << 20),
        name="finish",
    )(new_obj, new_probe, loss_mean)


def body(object_slab, probe_field, patterns, offsets, counts):
    ext, probe, pats, left, left_t, right, right_t, gext, pg, peak = halo(object_slab, probe_field, patterns)
    gext, pg, loss = compute(
        counts, jnp.swapaxes(offsets, 1, 2), ext, probe, pats, left, left_t, right, right_t, gext, pg
    )
    new_obj, new_probe, loss_mean = finish(*exchange(gext, pg, ext, probe, peak, loss))
    return new_obj, new_probe.reshape(probe_field.shape), loss_mean.reshape(())


def solution(mesh):
    placed = (
        P(None, "row", "col"),
        P(),
        P(("row", "col"), None, None, None),
        P(("row", "col"), None, None),
        P(),
    )
    return jax.shard_map(
        body,
        mesh=mesh,
        in_specs=placed,
        out_specs=(P(None, "row", "col"), P(), P()),
        check_vma=False,
    )
```

```python
import math

import jax
import jax.numpy as jnp
import ml_dtypes
import numpy as np
from jax import lax
from jax.experimental import pallas as pl
from jax.experimental.pallas import tpu as pltpu
from jax.sharding import PartitionSpec as P

N = 256
H = 128


def split(x):
    hi = x.astype(jnp.bfloat16)
    lo = (x - hi.astype(jnp.float32)).astype(jnp.bfloat16)
    return hi, lo

def tables():
    k = np.arange(H)[:, None]
    n = np.arange(H)[None, :]
    out = []
    for q in (0, 1):
        ph = -2.0 * math.pi * ((n * (2 * k + q)) % N) / N
        c, s = np.cos(ph) / 16.0, np.sin(ph) / 16.0
        out.append(np.block([[c, -s], [s, c]]))
    t = np.stack(out).astype(np.float32)
    def hl(a):
        hi = a.astype(ml_dtypes.bfloat16)
        lo = (a - hi.astype(np.float32)).astype(ml_dtypes.bfloat16)
        return hi, lo
    hi, lo = hl(t)
    left = np.concatenate([hi, hi, lo], axis=2)
    hiT, loT = hi.transpose(0, 2, 1), lo.transpose(0, 2, 1)
    leftT = np.concatenate([hiT, hiT, loT], axis=2)
    right = np.concatenate([hi, hi, lo], axis=1)
    rightT = np.concatenate([hiT, hiT, loT], axis=1)
    perm = np.zeros((N, N), np.float32)
    for i in range(H):
        perm[2 * i, i] = 1; perm[2 * i + 1, H + i] = 1
    return left, leftT, right, rightT, perm.astype(ml_dtypes.bfloat16)

def dot(a, b):
    return jnp.dot(a, b, preferred_element_type=jnp.float32)

def lmul(t, x):
    hi, lo = split(x)
    return dot(t, jnp.concatenate([hi, lo, hi], axis=0))

def rmul(x, t):
    hi, lo = split(x)
    return dot(jnp.concatenate([hi, lo, hi], axis=1), t)

def twice(a, axis):
    return jnp.concatenate([a, lax.slice_in_dim(a, 0, N, axis=axis)], axis=axis)


def compute_kernel(counts, offsets, ext, probe, pats, left, leftT, right, rightT, gext_in, pgrad_in,
                   gext, pgrad, loss_ref, patch, psi, res, acc, xa, xb, xc, xd):
    row = lax.axis_index("row")
    col = lax.axis_index("col")
    count = counts[row * 16 + col]
    loss_ref[...] = jnp.zeros_like(loss_ref)

    def slot(s, _):
        r = offsets[0, 0, s]
        c = offsets[0, 1, s]
        ca = pl.multiple_of(c // 128 * 128, 128)
        cs = c - ca
        ra = pl.multiple_of(r // 8 * 8, 8)
        rs = r - ra
        sub = lax.broadcasted_iota(jnp.int32, (1, 8, H), 1)
        lane = lax.broadcasted_iota(jnp.int32, (1, H), 1)
        for comp in (0, 1):
            x = ext[comp, pl.ds(ra, 264), pl.ds(ca, 384)]
            x = [pltpu.roll(x[:, i * H : i * H + H], H - cs, 1) for i in range(3)]
            for i in range(2):
                y = jnp.where(lane < H - cs, x[i], x[i + 1]).reshape(33, 8, H)
                y = pltpu.roll(y, 8 - rs, 1)
                patch[comp, :, i * H : i * H + H] = jnp.where(sub < 8 - rs, y[:32], y[1:]).reshape(N, H)

        def stage_a(m):
            for i in range(0, H, 16):
                er, ei = [], []
                for t in (i, H + i):
                    qr, qi = probe[0, m, t : t + 16], probe[1, m, t : t + 16]
                    xr, xi = patch[0, t : t + 16], patch[1, t : t + 16]
                    er.append(qr * xr - qi * xi)
                    ei.append(qr * xi + qi * xr)
                for p in (0, 1):
                    for at, e in ((i, er), (H + i, ei)):
                        hi, lo = split(e[0] + e[1] if p == 0 else e[0] - e[1])
                        xa[m % 2, p, at : at + 16] = hi
                        xa[m % 2, p, N + at : N + at + 16] = lo

        def stage_b(m):
            return [dot(left[p], twice(xa[m % 2, p], 0)) for p in (0, 1)]

        def stage_c(m, L):
            for p in (0, 1):
                for i in range(0, H, 16):
                    re, im = L[p][i : i + 16], L[p][H + i : H + i + 16]
                    at = slice(p * H + i, p * H + i + 16)
                    for q in (0, 1):
                        for lane, e in ((0, re), (H, im)):
                            f = e[:, :H] + e[:, H:] if q == 0 else e[:, :H] - e[:, H:]
                            hi, lo = split(f)
                            xb[m % 2, q, at, lane : lane + H] = hi
                            xb[m % 2, q, at, N + lane : N + lane + H] = lo

        def stage_d(m):
            return [dot(twice(xb[m % 2, q], 1), rightT[q]) for q in (0, 1)]

        def stage_e(m, X):
            for q in (0, 1):
                for i in range(0, N, 16):
                    x = X[q][i : i + 16]
                    psi[m, q, i : i + 16] = x
                    e = x[:, :H] * x[:, :H] + x[:, H:] * x[:, H:]
                    before = -pats[s, q, i : i + 16] if m == 0 else res[q, i : i + 16]
                    res[q, i : i + 16] = before + e

        Ls, Xs = {}, {}
        stage_a(0)
        for t in range(6):
            if t < 4:
                Ls[t] = stage_b(t)
            if 0 <= t - 1 < 4:
                Xs[t - 1] = stage_d(t - 1)
            if t + 1 < 4:
                stage_a(t + 1)
            if t < 4:
                stage_c(t, Ls[t])
            if 0 <= t - 1 < 4:
                stage_e(t - 1, Xs[t - 1])

        def stage_f(m):
            for q in (0, 1):
                for i in range(0, N, 16):
                    w = res[q, i : i + 16]
                    x = psi[m, q, i : i + 16]
                    for lane in (0, H):
                        hi, lo = split(x[:, lane : lane + H] * w)
                        xc[m % 2, q, i : i + 16, lane : lane + H] = hi
                        xc[m % 2, q, i : i + 16, N + lane : N + lane + H] = lo

        def stage_g(m):
            return [dot(twice(xc[m % 2, q], 1), right[q]) for q in (0, 1)]

        def stage_i(m, T):
            for p in (0, 1):
                for i in range(0, H, 16):
                    t0, t1 = T[0][p * H + i : p * H + i + 16], T[1][p * H + i : p * H + i + 16]
                    for half, x in ((0, t0 + t1), (H, t0 - t1)):
                        for at, lane in ((i, 0), (H + i, H)):
                            hi, lo = split(x[:, lane : lane + H])
                            xd[m % 2, p, at : at + 16, half : half + H] = hi
                            xd[m % 2, p, N + at : N + at + 16, half : half + H] = lo

        def stage_j(m):
            return [dot(leftT[p], twice(xd[m % 2, p], 0)) for p in (0, 1)]

        def stage_k(m, L):
            for i in range(0, H, 8):
                for h, sign in ((0, 1), (H, -1)):
                    at = slice(h + i, h + i + 8)
                    if sign == 1:
                        br = L[0][i : i + 8] + L[1][i : i + 8]
                        bi = L[0][H + i : H + i + 8] + L[1][H + i : H + i + 8]
                    else:
                        br = L[0][i : i + 8] - L[1][i : i + 8]
                        bi = L[0][H + i : H + i + 8] - L[1][H + i : H + i + 8]
                    qr, qi = probe[0, m, at], probe[1, m, at]
                    xr, xi = patch[0, at], patch[1, at]
                    gr, gi = qr * br + qi * bi, qr * bi - qi * br
                    if m:
                        gr, gi = acc[0, at] + gr, acc[1, at] + gi
                    acc[0, at] = gr
                    acc[1, at] = gi
                    pgrad[0, m, at] += xr * br + xi * bi
                    pgrad[1, m, at] += xr * bi - xi * br

        Ts, Ls = {}, {}
        stage_f(0)
        loss_ref[...] += jnp.sum((res[0] * res[0] + res[1] * res[1]).reshape(32, 8, 128), axis=0)
        for t in range(6):
            if t < 4:
                Ts[t] = stage_g(t)
            if 0 <= t - 1 < 4:
                Ls[t - 1] = stage_j(t - 1)
            if t + 1 < 4:
                stage_f(t + 1)
            if t < 4:
                stage_i(t, Ts[t])
            if 0 <= t - 1 < 4:
                stage_k(t - 1, Ls[t - 1])

        for comp in (0, 1):
            none = jnp.zeros((1, 8, H), jnp.float32)
            blank = jnp.zeros((264, H), jnp.float32)
            x = []
            for i in range(2):
                y = pltpu.roll(acc[comp, :, i * H : i * H + H].reshape(32, 8, H), rs, 1)
                y = jnp.where(sub < rs, jnp.concatenate([none, y], axis=0), jnp.concatenate([y, none], axis=0))
                x.append(pltpu.roll(y.reshape(264, H), cs, 1))
            x = [blank, x[0], x[1], blank]
            for i in range(3):
                at = pl.ds(pl.multiple_of(ca + i * H, H), H)
                gext[comp, pl.ds(ra, 264), at] += jnp.where(lane < cs, x[i], x[i + 1])
        return 0

    lax.fori_loop(0, count, slot, 0)
    scans = lax.fori_loop(0, counts.shape[0], lambda i, t: t + counts[i], 0)
    loss_ref[...] = loss_ref[...] * (0.5 / (scans.astype(jnp.float32) * (N * N)))

    @pl.when(col == 15)
    def _():
        gext[:, :, 2 * N : 3 * N] = jnp.zeros((2, 776, N), jnp.float32)

    @pl.when(row == 7)
    def _():
        gext[:, 2 * N : 3 * N, :] = jnp.zeros((2, N, 896), jnp.float32)


def compute(counts, offsets, ext, probe, pats, *consts):
    V = pl.BlockSpec(memory_space=pltpu.VMEM)
    S = pl.BlockSpec(memory_space=pltpu.SMEM)
    return pl.pallas_call(
        compute_kernel,
        out_shape=(
            pltpu.VMEM((2, 776, 896), jnp.float32),
            pltpu.VMEM((2, 4, N, N), jnp.float32),
            jax.ShapeDtypeStruct((8, 128), jnp.float32),
        ),
        in_specs=[S, S] + [V] * 9,
        out_specs=(V, V, V),
        input_output_aliases={9: 0, 10: 1},
        scratch_shapes=[
            pltpu.VMEM((2, N, N), jnp.float32),
            pltpu.VMEM((4, 2, N, N), jnp.float32),
            pltpu.VMEM((2, N, H), jnp.float32),
            pltpu.VMEM((2, N, N), jnp.float32),
            pltpu.VMEM((2, 2, 2 * N, N), jnp.bfloat16),
            pltpu.VMEM((2, 2, N, 2 * N), jnp.bfloat16),
            pltpu.VMEM((2, 2, N, 2 * N), jnp.bfloat16),
            pltpu.VMEM((2, 2, 2 * N, N), jnp.bfloat16),
        ],
        compiler_params=pltpu.CompilerParams(vmem_limit_bytes=16 << 20),
        name="compute",
    )(counts, offsets, ext, probe, pats, *consts)


MESH = pl.DeviceIdType.MESH
F32 = jnp.float32


def place():
    row = lax.axis_index("row")
    col = lax.axis_index("col")
    return col // 4, row // 2, col % 4, row % 2


def device_at(x, y, z, k):
    return (lax.rem(y + 8, 4) * 2 + k, lax.rem(x + 8, 4) * 4 + lax.rem(z + 8, 4))


def neighbours():
    row = lax.axis_index("row")
    col = lax.axis_index("col")
    left = (row, lax.rem(col + 15, 16))
    right = (row, lax.rem(col + 1, 16))
    above = (lax.rem(row + 7, 8), col)
    below = (lax.rem(row + 1, 8), col)
    return left, right, above, below


def groups():
    x, y, z, k = place()
    return {
        "k": [device_at(x, y, z, 1 - k)],
        "x": [device_at(x + d, y, z, k) for d in (1, 2, 3)],
        "y": [device_at(x, y + d, z, k) for d in (1, 2, 3)],
        "z": [device_at(x, y, z + d, k) for d in (1, 2, 3)],
    }


def greet(peers):
    barrier = pltpu.get_barrier_semaphore()
    for peer in peers:
        pl.semaphore_signal(barrier, inc=1, device_id=peer, device_id_type=MESH)
    pl.semaphore_wait(barrier, len(peers))


def remote(src, dst, send, recv, i, peer):
    copy = pltpu.make_async_remote_copy(
        src_ref=src, dst_ref=dst, send_sem=send.at[i], recv_sem=recv.at[i], device_id=peer, device_id_type=MESH
    )
    copy.start()
    return copy


class Small:
    def __init__(self, op, value, slots, send, recv, base):
        self.op, self.value, self.slots, self.send, self.recv, self.base = op, value, slots, send, recv, base
        self.step, self.at = 0, 0
        self.done = []

    def start(self):
        axis = "kxyz"[self.step]
        mine = dict(zip("xyzk", place()))[axis]
        self.slots[self.step, mine] = self.value[self.step]
        self.copies = []
        for peer in groups()[axis]:
            self.copies.append(
                remote(
                    self.value.at[self.step], self.slots.at[self.step, mine], self.send, self.recv,
                    self.base + self.at, peer,
                )
            )
            self.at += 1

    def finish(self):
        for copy in self.copies:
            copy.wait_recv()
        self.done += self.copies
        total = self.slots[self.step, 0]
        for i in range(1, len(self.copies) + 1):
            total = self.op(total, self.slots[self.step, i])
        self.step += 1
        self.value[self.step] = total


def halo_kernel(obj, probe, patterns, left_t, left_tt, right_t, right_tt, perm,
                ext, probe_v, pat_v, left_v, left_tv, right_v, right_tv, gext, pgrad, peak,
                raw, sort, swap, relay, local, send, recv):
    n = 256
    west, east, above, below = neighbours()
    x, y, z, k = place()
    up = device_at(x, y, z + 1, k)
    down = device_at(x, y, z - 1, k)
    end = device_at(x - jnp.where(z == 2, 1, 0), y, z + 1, k)
    origin = device_at(x + jnp.where(z == 3, 1, 0), y, z - 1, k)
    pairs = [
        (probe, probe_v), (patterns.at[0], raw), (perm, sort), (left_t, left_v), (left_tt, left_tv),
        (right_t, right_v), (right_tt, right_tv), (obj, ext.at[:, 0 : 2 * n, 0 : 2 * n]),
    ]
    loads = [pltpu.make_async_copy(src, dst, local.at[i]) for i, (src, dst) in enumerate(pairs)]
    greet([west, east, above, below, up, down, end, origin])
    top = [
        remote(obj.at[:, m : m + H, 0:n], ext.at[:, m : m + H, 2 * n : 3 * n], send, recv, i, west)
        for i, m in ((0, 0), (3, H))
    ]
    side = remote(obj.at[:, 0:n, :], ext.at[:, 2 * n : 3 * n, 0 : 2 * n], send, recv, 2, above)
    first = [
        remote(obj.at[:, 384 + 64 * i : 448 + 64 * i, 0:n], relay.at[0, i], send, recv, 4 + i, up) for i in (0, 1)
    ]
    middle = remote(obj.at[:, n:384, 0:n], ext.at[:, n:384, 2 * n : 3 * n], send, recv, 1, west)
    for load in loads:
        load.start()
    gext[...] = jnp.zeros_like(gext)
    pgrad[...] = jnp.zeros_like(pgrad)
    for load in loads:
        load.wait()

    def largest(i, best):
        at = pl.ds(pl.multiple_of(i * 16, 16), 16)
        re = ext[0, at, 0 : 2 * n]
        im = ext[1, at, 0 : 2 * n]
        return jnp.maximum(best, re * re + im * im)

    best = lax.fori_loop(0, 32, largest, jnp.zeros((16, 512), F32))
    peak[...] = jnp.full((8, 128), jnp.max(best), F32)

    def order(s, _):
        hi, lo = split(raw[s])
        both = dot(hi, sort[...]) + dot(lo, sort[...])
        for q in (0, 1):
            swap[q] = both[:, q * H : (q + 1) * H]
        for q in (0, 1):
            for p in (0, 1):
                pat_v[s, q, p * H : (p + 1) * H, :] = swap[q, pl.ds(p, H, stride=2), :]
        return 0

    lax.fori_loop(0, 4, order, 0)
    second, corner = [], []
    for i in (0, 1):
        first[i].wait_recv()
        second.append(remote(relay.at[0, i], relay.at[1, i], send, recv, 6 + i, up))
        top[i].wait_recv()
        m = i * H
        corner.append(
            remote(
                ext.at[:, m : m + H, 2 * n : 3 * n], ext.at[:, 2 * n + m : 2 * n + m + H, 2 * n : 3 * n],
                send, recv, 10 + i, above,
            )
        )
    third = []
    for i in (0, 1):
        second[i].wait_recv()
        m = pl.ds(384 + 64 * i, 64)
        third.append(remote(relay.at[1, i], ext.at[:, m, 2 * n : 3 * n], send, recv, 8 + i, end))
    for copy in (side, middle, *corner, *third):
        copy.wait_recv()
    for copy in (*top, side, middle, *corner, *first, *second, *third):
        copy.wait_send()

    @pl.when(lax.axis_index("col") == 15)
    def _():
        ext[:, :, 2 * n : 3 * n] = jnp.zeros((2, 776, n), F32)

    @pl.when(lax.axis_index("row") == 7)
    def _():
        ext[:, 2 * n : 3 * n, :] = jnp.zeros((2, n, 896), F32)


def halo(obj, probe, patterns):
    V = pl.BlockSpec(memory_space=pltpu.VMEM)
    A = pl.BlockSpec(memory_space=pltpu.HBM)
    consts = [jnp.asarray(t) for t in tables()]
    ins = [pltpu.with_memory_space_constraint(t, pltpu.HBM) for t in (obj, probe, patterns, *consts)]
    shapes = [(2, 776, 896), (2, 4, N, N), (4, 2, N, H)]
    outs = [pltpu.VMEM(s, F32) for s in shapes] + [pltpu.VMEM(t.shape, t.dtype) for t in consts[:4]]
    outs += [pltpu.VMEM(s, F32) for s in shapes[:2]]
    return pl.pallas_call(
        halo_kernel,
        out_shape=tuple(outs) + (jax.ShapeDtypeStruct((8, 128), F32),),
        in_specs=[A] * 8,
        out_specs=(V,) * 10,
        scratch_shapes=[
            pltpu.VMEM((4, N, N), F32),
            pltpu.VMEM((N, N), jnp.bfloat16),
            pltpu.VMEM((2, N, H), F32),
            pltpu.VMEM((2, 2, 2, 64, N), F32),
            pltpu.SemaphoreType.DMA((8,)),
            pltpu.SemaphoreType.DMA((12,)),
            pltpu.SemaphoreType.DMA((12,)),
        ],
        compiler_params=pltpu.CompilerParams(collective_id=0, has_side_effects=True, vmem_limit_bytes=16 << 20),
        name="halo",
    )(*ins)


PARTS = ((0, 128, "xyz"), (128, 128, "yzx"), (256, 128, "zxy"), (384, 256, "xyz"), (640, 128, "yzx"), (768, 256, "zxy"))


def exchange_kernel(gext, pg, probe, peak, loss, over, side, inverse, new_probe, loss_mean,
                    strip, corner, relay, r0, r1, r2, rz, value, slots, send, recv):
    n = 256
    left, right, above, below = neighbours()
    group = groups()
    x, y, z, k = place()
    index = {"x": x, "y": y, "z": z, "k": k}
    up, down = device_at(x, y, z + 1, k), device_at(x, y, z - 1, k)
    end = device_at(x + jnp.where(z == 1, 1, 0), y, z - 1, k)
    origin = device_at(x - jnp.where(z == 0, 1, 0), y, z + 1, k)
    counter = [0]

    def push(src, dst, peer):
        counter[0] += 1
        return remote(src, dst, send, recv, counter[0] - 1, peer)

    def rows(start, size):
        return pl.ds(pl.multiple_of(start, 8), size)

    def op(a, b):
        first = lax.broadcasted_iota(jnp.int32, (16, 128), 0) < 8
        return jnp.where(first, a + b, jnp.maximum(a, b))

    everyone = [group[a][i] for a in "kxyz" for i in range(len(group[a]))] + [left, right, above, below, up, down, end, origin]
    greet(everyone)
    sent = []
    over_sent, side_sent, corner_sent, rounds = [], [], [], ([], [], [])

    def push_corner(i):
        m = pl.ds(2 * n + 128 * i, 128)
        corner_sent.append(push(gext.at[:, m, 2 * n : 3 * n], corner.at[:, 128 * i : 128 * i + 128], below))

    def push_over(i):
        m = pl.ds(2 * n + 64 * i, 64)
        over_sent.append(push(gext.at[:, m, 0 : 2 * n], over.at[:, 64 * i : 64 * i + 64], below))

    def push_side(i):
        m = pl.ds(n + 64 * i, 64) if i < 2 else pl.ds(64 * i - 128, 64)
        source = gext.at[:, m, 2 * n : 3 * n] if i < 2 else strip.at[:, m]
        side_sent.append(push(source, side.at[:, m], right))

    def push_round(step, i):
        m = pl.ds(384 + 64 * i, 64)
        source = gext.at[:, m, 2 * n : 3 * n] if step == 0 else relay.at[step - 1, i]
        target = side.at[:, m] if step == 2 else relay.at[step, i]
        if step:
            rounds[step - 1][i].wait_recv()
        rounds[step].append(push(source, target, end if step == 2 else down))

    def fold_corner(i):
        corner_sent[i].wait_recv()
        m = pl.ds(128 * i, 128)
        strip[:, m] = gext[:, m, 2 * n : 3 * n] + corner[:, m]

    swap = []
    for first, size, _ in PARTS:
        swap.append(push(pg.at[rows((1 - k) * 1024 + first, size)], r0.at[first : first + size], group["k"][0]))
    push_corner(0)
    push_side(0)
    push_round(0, 0)
    value[0, 0:8] = loss[...]
    value[0, 8:16] = peak[...]
    small = Small(op, value, slots, send, recv, 200)
    small.start()

    steps = []
    for p, (first, size, axes) in enumerate(PARTS):
        swap[p].wait_recv()
        r0[first : first + size] += pg[rows(k * 1024 + first, size)]
        q = size // 4
        a = axes[0]
        copies = []
        for d, peer in enumerate(group[a]):
            other = lax.rem(index[a] + d + 1, 4)
            copies.append(push(r0.at[rows(first + other * q, q)], r1.at[d, first // 4 : first // 4 + q], peer))
        steps.append(copies)
    small.finish()
    small.start()
    push_corner(1)
    push_side(1)
    push_round(0, 1)
    second = []
    for p, (first, size, axes) in enumerate(PARTS):
        q, e = size // 4, size // 16
        a, b, c = axes
        f1, f2 = first // 4, first // 16
        for copy in steps[p]:
            copy.wait_recv()
        sent += steps[p]
        mine = rows(first + index[a] * q, q)
        r0[mine] += r1[0, f1 : f1 + q] + r1[1, f1 : f1 + q] + r1[2, f1 : f1 + q]
        copies = []
        for d, peer in enumerate(group[b]):
            other = lax.rem(index[b] + d + 1, 4)
            copies.append(push(r0.at[rows(first + index[a] * q + other * e, e)], r2.at[d, f2 : f2 + e], peer))
        second.append(copies)
    small.finish()
    small.start()
    push_over(0)
    fold_corner(0)
    push_side(2)
    push_round(1, 0)
    push_round(1, 1)
    third = []
    for p, (first, size, axes) in enumerate(PARTS):
        q, e = size // 4, size // 16
        a, b, c = axes
        f2 = first // 16
        for copy in second[p]:
            copy.wait_recv()
        sent += second[p]
        mine = rows(first + index[a] * q + index[b] * e, e)
        total = r0[mine] + r2[0, f2 : f2 + e] + r2[1, f2 : f2 + e] + r2[2, f2 : f2 + e]
        r0[mine] = total
        rz[index[c], f2 : f2 + e] = total
        third.append([push(r0.at[mine], rz.at[index[c], f2 : f2 + e], peer) for peer in group[c]])
    small.finish()
    small.start()
    push_over(1)
    fold_corner(1)
    push_side(3)
    small.finish()
    loss_mean[0, 0] = jnp.sum(value[4, 0:8])
    scale = 1.0 / value[4, 8:9, 0:1]

    back = []
    for p, (first, size, axes) in enumerate(PARTS):
        q, e = size // 4, size // 16
        a, b, c = axes
        f2 = first // 16
        for copy in third[p]:
            copy.wait_recv()
        sent += third[p]
        mine = rows(k * 1024 + first + index[a] * q + index[b] * e, e)
        total = ((rz[0, f2 : f2 + e] + rz[1, f2 : f2 + e]) + rz[2, f2 : f2 + e]) + rz[3, f2 : f2 + e]
        new_probe[mine] = probe[mine] - total * scale
        back.append([push(new_probe.at[mine], new_probe.at[mine], peer) for peer in group[b]])
    push_over(2)
    push_side(4)
    push_round(2, 0)
    push_round(2, 1)
    last = []
    for p, (first, size, axes) in enumerate(PARTS):
        q, e = size // 4, size // 16
        a, b, c = axes
        copies = []
        for d in range(4):
            if d:
                back[p][d - 1].wait_recv()
            mine = rows(k * 1024 + first + index[a] * q + lax.rem(index[b] + 4 - d, 4) * e, e)
            copies.append([push(new_probe.at[mine], new_probe.at[mine], peer) for peer in group[a]])
        sent += back[p]
        last.append(copies)
    push_over(3)
    push_side(5)
    probe_peak = jnp.max(sum(probe[m * n : (m + 1) * n] * probe[m * n : (m + 1) * n] for m in range(8)))
    inverse[...] = jnp.full((8, 128), 1.0 / probe_peak, F32)
    final = []
    for p, (first, size, axes) in enumerate(PARTS):
        q = size // 4
        a, b, c = axes
        for d in range(4):
            if d:
                for copies in last[p]:
                    copies[d - 1].wait_recv()
            mine = rows(k * 1024 + first + lax.rem(index[a] + 4 - d, 4) * q, q)
            final.append(push(new_probe.at[mine], new_probe.at[mine], group["k"][0]))
        for copies in last[p]:
            sent += copies
    for copy in over_sent:
        copy.wait_recv()
    for copy in side_sent + rounds[2]:
        copy.wait_recv()
    sent += over_sent + side_sent + rounds[0] + rounds[1] + rounds[2] + corner_sent + swap + final + small.done
    for copy in final:
        copy.wait_recv()
    for copy in sent:
        copy.wait_send()


def exchange(gext, pg, probe, peak, loss):
    V = pl.BlockSpec(memory_space=pltpu.VMEM)
    S = pl.BlockSpec(memory_space=pltpu.SMEM)
    return pl.pallas_call(
        exchange_kernel,
        out_shape=(
            pltpu.VMEM((2, 256, 512), F32),
            pltpu.VMEM((2, 512, 256), F32),
            pltpu.VMEM((8, 128), F32),
            pltpu.VMEM((2048, 256), F32),
            jax.ShapeDtypeStruct((1, 1), F32),
        ),
        in_specs=[V] * 5,
        out_specs=(V, V, V, V, S),
        scratch_shapes=[
            pltpu.VMEM((2, 256, 256), F32),
            pltpu.VMEM((2, 256, 256), F32),
            pltpu.VMEM((2, 2, 2, 64, 256), F32),
            pltpu.VMEM((1024, 256), F32),
            pltpu.VMEM((3, 256, 256), F32),
            pltpu.VMEM((3, 64, 256), F32),
            pltpu.VMEM((4, 64, 256), F32),
            pltpu.VMEM((5, 16, 128), F32),
            pltpu.VMEM((4, 4, 16, 128), F32),
            pltpu.SemaphoreType.DMA((212,)),
            pltpu.SemaphoreType.DMA((212,)),
        ],
        compiler_params=pltpu.CompilerParams(collective_id=1, has_side_effects=True, vmem_limit_bytes=30 << 20),
        name="exchange",
    )(gext, pg.reshape(2048, 256), probe.reshape(2048, 256), peak, loss)


def finish_kernel(gext, obj, over, side, inverse, new_probe, loss_mean, obj_out, probe_out, loss_out, new_obj, sems):
    n = 256
    copies = []
    for i in range(4):
        m = pl.ds(512 * i, 512)
        copies.append(pltpu.make_async_copy(new_probe.at[m], probe_out.at[m], sems.at[4 + i]))
        copies[-1].start()
    loss_out[0, 0] = loss_mean[0, 0]
    scale = inverse[0:1, 0:1]
    for i in range(4):
        m = pl.ds(128 * i, 128)
        left = gext[:, m, 0:n] + side[:, m]
        right = gext[:, m, n : 2 * n]
        if i < 2:
            left += over[:, m, 0:n]
            right += over[:, m, n : 2 * n]
        new_obj[:, m, 0:n] = obj[:, m, 0:n] - left * scale
        new_obj[:, m, n : 2 * n] = obj[:, m, n : 2 * n] - right * scale
        copies.append(pltpu.make_async_copy(new_obj.at[:, m], obj_out.at[:, m], sems.at[i]))
        copies[-1].start()
    for copy in copies:
        copy.wait()


def finish(gext, obj, over, side, inverse, new_probe, loss_mean):
    V = pl.BlockSpec(memory_space=pltpu.VMEM)
    A = pl.BlockSpec(memory_space=pltpu.HBM)
    S = pl.BlockSpec(memory_space=pltpu.SMEM)
    return pl.pallas_call(
        finish_kernel,
        out_shape=(
            pltpu.HBM((2, 512, 512), F32),
            pltpu.HBM(new_probe.shape, F32),
            jax.ShapeDtypeStruct((1, 1), F32),
        ),
        in_specs=[V] * 6 + [S],
        out_specs=(A, A, S),
        scratch_shapes=[pltpu.VMEM((2, 512, 512), F32), pltpu.SemaphoreType.DMA((8,))],
        compiler_params=pltpu.CompilerParams(vmem_limit_bytes=8 << 20),
        name="finish",
    )(gext, obj, over, side, inverse, new_probe, loss_mean)


def body(object_slab, probe_field, patterns, offsets, counts):
    ext, probe, pats, left, left_t, right, right_t, gext, pg, peak = halo(object_slab, probe_field, patterns)
    gext, pg, loss = compute(
        counts, jnp.swapaxes(offsets, 1, 2), ext, probe, pats, left, left_t, right, right_t, gext, pg
    )
    new_obj, new_probe, loss_mean = finish(gext, ext, *exchange(gext, pg, probe, peak, loss))
    return new_obj, new_probe.reshape(probe_field.shape), loss_mean.reshape(())


def solution(mesh):
    placed = (
        P(None, "row", "col"),
        P(),
        P(("row", "col"), None, None, None),
        P(("row", "col"), None, None),
        P(),
    )
    return jax.shard_map(
        body,
        mesh=mesh,
        in_specs=placed,
        out_specs=(P(None, "row", "col"), P(), P()),
        check_vma=False,
    )
```
